256 devices in a mesh: seq: 64 (over z, x, core), head: 4 (over y).
Axes of the slice: x: 4, y: 4, z: 8, core: 2. Of those that a mesh axis runs over, the one named last changes fastest.
Arguments:
- queries: bfloat16 [32768, 4096], P('seq', 'head'), may hold values from -15 to 15
- keys: bfloat16 [32768, 4096], P('seq', 'head'), may hold values from -15 to 15
- values: bfloat16 [32768, 4096], P('seq', 'head'), may hold values from -6 to 6
- offsets_b: int32 [8, 32], P(None, 'head'), may hold values from 0 to 3
- offsets_c: int32 [32], P('head'), may hold values from 0 to 31
- out_weight: bfloat16 [4096, 4096], P(None, 'head'), may hold values from -0.09375 to 0.09375
Outputs:
- mixed: bfloat16 [32768, 4096], P('seq', 'head')
The draws below stay inside these ranges and needn't reach their ends.
All inputs are finite; a program needn't handle non-finite values.
Results may differ from the reference program's by a relative error of at most 0.0054.
Values may be sent and summed in bfloat16 or wider, within the bound.
A program may use at most 128 MiB of HBM per device.

```python
import jax
import jax.numpy as jnp
from jax import lax

HEADS = 32
HEAD_DIM = 128
D = 4096
RATE_B = 4
TOKENS = 32768
SEG_A = 1024
SEG_B = 4096
SEGS_B = 8
RATE_C = 32


def draw_queries(key, part):
    key = jax.random.fold_in(key, 3)
    result = jnp.clip(jax.random.normal(key, (TOKENS, HEADS * HEAD_DIM), jnp.float32), -6.0, 6.0)
    return result.astype(jnp.bfloat16)


def draw_keys(key, part):
    key = jax.random.fold_in(key, 4)
    result = jnp.clip(jax.random.normal(key, (TOKENS, HEADS * HEAD_DIM), jnp.float32), -6.0, 6.0)
    return result.astype(jnp.bfloat16)


def touch_ends(drawn, stream_key, smallest, high):
    spot = [jax.random.randint(jax.random.fold_in(stream_key, axis), (), 0, length) for axis, length in enumerate(drawn.shape)]
    widest = drawn.shape.index(max(drawn.shape))
    beside = spot[:widest] + [(spot[widest] + 1) % drawn.shape[widest]] + spot[widest + 1:]
    return drawn.at[tuple(spot)].set(smallest).at[tuple(beside)].set(high)


def steps_of(rng, dims, pieces, least, high):
    loudness, own = 1.0, jax.random.fold_in(rng, 6)
    for axis_at, parts in pieces:
        heights = jnp.exp(jax.random.uniform(jax.random.fold_in(own, axis_at), (parts,), jnp.float32, least / len(pieces), high / len(pieces)))
        loudness = loudness * jnp.repeat(heights, dims[axis_at] // parts).reshape([-1 if axis == axis_at else 1 for axis in range(len(dims))])
    return loudness


def centred(rng, dims, deviation, bound, split=(), kind=jnp.bfloat16):
    values = deviation * jax.random.normal(rng, dims, jnp.float32)
    if split:
        values = values * steps_of(rng, dims, split, -0.22, 0.18)
    return jnp.clip(values, -bound, bound).astype(kind)


def setup_inputs(seed: int = 0) -> dict:
    key_list = jax.random.split(jax.random.key(seed), 7)
    queries = draw_queries(jax.random.fold_in(key_list[6], 71), 0)
    keys = draw_keys(jax.random.fold_in(key_list[6], 71), 0)
    values = centred(key_list[2], (TOKENS, HEADS * HEAD_DIM), 1.0, 6.0, ((0, 64), (1, 4)))
    offsets_b = touch_ends(jax.random.randint(key_list[3], (SEGS_B, HEADS), 0, RATE_B), jax.random.fold_in(key_list[3], 1), 0, RATE_B - 1).astype(jnp.int32)
    offsets_c = touch_ends(jax.random.randint(key_list[4], (HEADS,), 0, RATE_C), jax.random.fold_in(key_list[4], 1), 0, RATE_C - 1).astype(jnp.int32)
    out_weight = centred(key_list[5], (HEADS * HEAD_DIM, D), (HEADS * HEAD_DIM) ** -0.5, 0.09375, ((1, 4),))
    return {"queries": queries, "keys": keys, "values": values, "offsets_b": offsets_b, "offsets_c": offsets_c, "out_weight": out_weight}


masked_score = -1.0e30


def attend(query_sub, key_sub, value_sub, allowed):
    score_scale = float(HEAD_DIM) ** -0.5
    scores = jnp.einsum("ihd,jhd->hij", query_sub.astype(jnp.float32), key_sub.astype(jnp.float32)) * score_scale
    scores = jnp.where(allowed[None], scores, masked_score)
    row_top = jnp.max(scores, axis=2)
    weights = jnp.exp(scores - row_top[:, :, None])
    weight_sum = jnp.sum(weights, axis=2)
    numerator = jnp.einsum("hij,jhd->ihd", weights.astype(jnp.bfloat16).astype(jnp.float32), value_sub.astype(jnp.float32))
    return row_top.T, weight_sum.T, numerator


def select(field, offset, stride):
    grouped = field.reshape(field.shape[0] // stride, stride, field.shape[1], field.shape[2])
    picked = jnp.arange(stride)[:, None] == offset[None, :]
    return jnp.sum(jnp.where(picked[None, :, :, None], grouped, jnp.zeros((), field.dtype)), axis=1).astype(field.dtype)


def spread(row_top, weight_sum, numerator, offset, stride):
    picked = (jnp.arange(stride)[:, None] == offset[None, :])[None]
    row_count = row_top.shape[0]
    heads_here = row_top.shape[1]
    chosen = jnp.broadcast_to(picked, (row_count, stride, heads_here)).reshape(row_count * stride, heads_here)
    top_full = jnp.where(picked, row_top[:, None, :], 0.0).reshape(row_count * stride, heads_here)
    sum_full = jnp.where(picked, weight_sum[:, None, :], 0.0).reshape(row_count * stride, heads_here)
    numer_full = jnp.where(picked[..., None], numerator[:, None], 0.0).reshape(row_count * stride, heads_here, numerator.shape[2])
    return chosen, top_full, sum_full, numer_full


def level_out(query_seg, key_seg, value_seg, offset, stride):
    query_sub = select(query_seg, offset, stride)
    key_sub = select(key_seg, offset, stride)
    value_sub = select(value_seg, offset, stride)
    row_count = query_sub.shape[0]
    allowed = jnp.arange(row_count)[None, :] <= jnp.arange(row_count)[:, None]
    row_top, weight_sum, numerator = attend(query_sub, key_sub, value_sub, allowed)
    return spread(row_top, weight_sum, numerator, offset, stride)


def combine(levels):
    base_top = levels[0][1]
    peak = base_top
    for chosen, row_top, weight_sum, numerator in levels[1:]:
        peak = jnp.maximum(peak, jnp.where(chosen, row_top, base_top))
    numer_total = jnp.zeros(levels[0][3].shape, jnp.float32)
    denom_total = jnp.zeros(base_top.shape, jnp.float32)
    for chosen, row_top, weight_sum, numerator in levels:
        factor = jnp.where(chosen, jnp.exp(jnp.where(chosen, row_top, peak) - peak), 0.0)
        numer_total = numer_total + factor[..., None] * numerator
        denom_total = denom_total + factor * weight_sum
    return (numer_total / denom_total[..., None]).astype(jnp.bfloat16)


def reference(queries, keys, values, offsets_b, offsets_c, out_weight):
    query_all = queries.reshape(TOKENS, HEADS, HEAD_DIM)
    key_all = keys.reshape(TOKENS, HEADS, HEAD_DIM)
    value_all = values.reshape(TOKENS, HEADS, HEAD_DIM)
    zero_offset = jnp.zeros((HEADS,), jnp.int32)
    half_seg = SEG_A // 2

    def level_diag(parts_in):
        return level_out(parts_in[0], parts_in[1], parts_in[2], zero_offset, 1)

    shape_h = (TOKENS // half_seg, half_seg, HEADS, HEAD_DIM)
    outs_diag = lax.map(level_diag, (query_all.reshape(shape_h), key_all.reshape(shape_h), value_all.reshape(shape_h)))
    outs_diag = tuple(member.reshape((TOKENS,) + member.shape[2:]) for member in outs_diag)

    def level_cross(parts_in):
        allowed = jnp.ones((half_seg, half_seg), jnp.bool_)
        row_top, weight_sum, numerator = attend(parts_in[0][1], parts_in[1][0], parts_in[2][0], allowed)
        chosen = jnp.concatenate([jnp.zeros((half_seg, HEADS), jnp.bool_), jnp.ones((half_seg, HEADS), jnp.bool_)], 0)
        top_full = jnp.concatenate([jnp.zeros_like(row_top), row_top], 0)
        sum_full = jnp.concatenate([jnp.zeros_like(weight_sum), weight_sum], 0)
        numer_full = jnp.concatenate([jnp.zeros_like(numerator), numerator], 0)
        return chosen, top_full, sum_full, numer_full

    shape_p = (TOKENS // SEG_A, 2, half_seg, HEADS, HEAD_DIM)
    outs_cross = lax.map(level_cross, (query_all.reshape(shape_p), key_all.reshape(shape_p), value_all.reshape(shape_p)))
    outs_cross = tuple(member.reshape((TOKENS,) + member.shape[2:]) for member in outs_cross)

    def level_b(parts_in):
        return level_out(parts_in[0], parts_in[1], parts_in[2], parts_in[3], RATE_B)

    shape_b = (SEGS_B, SEG_B, HEADS, HEAD_DIM)
    outs_b = lax.map(level_b, (query_all.reshape(shape_b), key_all.reshape(shape_b), value_all.reshape(shape_b), offsets_b))
    outs_b = tuple(member.reshape((TOKENS,) + member.shape[2:]) for member in outs_b)
    outs_c = level_out(query_all, key_all, value_all, offsets_c, RATE_C)
    attended = combine([outs_diag, outs_cross, outs_b, outs_c]).reshape(TOKENS, HEADS * HEAD_DIM)
    return jnp.dot(attended, out_weight, preferred_element_type=jnp.float32).astype(jnp.bfloat16)
```

```python
import functools

import jax
import jax.numpy as jnp
from jax import lax
from jax.experimental import pallas as pl
from jax.experimental.pallas import tpu as pltpu
from jax.sharding import PartitionSpec as P

HEAD_DIM = 128
RATE_B = 4
LOG2E = 1.4426950408889634
NEG = -1e30
MESH = pl.DeviceIdType.MESH
F32 = jnp.float32
BF16 = jnp.bfloat16
NN = (((1,), (0,)), ((), ()))
NT = (((1,), (1,)), ((), ()))
TN = (((0,), (0,)), ((), ()))


def dot(a, b, dims=NN):
    return lax.dot_general(a, b, dims, preferred_element_type=F32)


def iota(shape, axis):
    return lax.broadcasted_iota(jnp.int32, shape, axis)


def one_hot(shape, condition):
    return jnp.where(condition, jnp.ones(shape, F32), jnp.zeros(shape, F32)).astype(BF16)


def late_other(b, c):
    residue = lax.rem(c, RATE_B)
    return jnp.where(residue == b, lax.rem(b + 1, RATE_B), residue)


def stat_rows(count, level):
    high = level.astype(BF16).astype(F32)
    rest = level - high
    mid = rest.astype(BF16).astype(F32)
    low = rest - mid
    row = iota((count, level.shape[1]), 0)
    zero = jnp.zeros((count, level.shape[1]), F32)
    return jnp.where(row == 0, high, jnp.where(row == 1, mid, jnp.where(row == 2, low, zero)))


def kernel(
    q_hbm, k_hbm, v_hbm, offs_b, offs_c, w_hbm, out_hbm,
    qv, kv, vv, mkv, wv, st1b, st1c, rc1b, rc1c, ckv, pm, pmt, oa, la,
    rbst, rbrc, rcst, rcrc, xs, xr, att, acc, outv, ost, orc, osm,
    ld_s, mate_ss, mate_rs, p1c_ss, p1c_rs, p1b_ss, p1b_rs, zg_ss, zg_rs,
    rb_ss, rb_rs, rc_ss, rc_rs, x_ss, x_rs, f_ss, of_ss, of_rs, os_s, out_s,
):
    rows, width = qv.shape
    heads = width // HEAD_DIM
    half = rows // 2
    sel_b = rows // RATE_B
    sel_c = st1c.shape[1]
    top_stride = rows // sel_c
    scale = HEAD_DIM**-0.5 * LOG2E

    s = lax.axis_index("seq")
    y = lax.axis_index("head")
    ny = lax.axis_size("head")
    nz = lax.axis_size("seq") // heads
    z = s // heads
    i = s % heads
    core = s % 2
    right = (y + 1) % ny
    left = (y + ny - 1) % ny

    def plane(j):
        return {"seq": z * heads + j}

    def along_z(t):
        return {"seq": t * heads + i}

    def remote(src, dst, ssem, rsem, device):
        return pltpu.make_async_remote_copy(
            src_ref=src, dst_ref=dst, send_sem=ssem, recv_sem=rsem, device_id=device, device_id_type=MESH
        )

    loads = [
        pltpu.make_async_copy(src, dst, ld_s.at[n])
        for n, (src, dst) in enumerate(((q_hbm, qv), (k_hbm, kv), (v_hbm, vv), (w_hbm, wv)))
    ]
    for copy in loads:
        copy.start()
    barrier = pltpu.get_barrier_semaphore()

    def greet_plane(d, _):
        pl.semaphore_signal(barrier, 1, device_id=plane((i + d) % heads), device_id_type=MESH)
        return 0

    def greet_z(d, _):
        pl.semaphore_signal(barrier, 1, device_id=along_z((z + d) % nz), device_id_type=MESH)
        return 0

    lax.fori_loop(1, heads, greet_plane, 0)
    lax.fori_loop(1, nz, greet_z, 0)
    for d in range(1, 4):
        pl.semaphore_signal(barrier, 1, device_id={"head": (y + d) % ny}, device_id_type=MESH)

    for r in range(RATE_B):
        pm[r] = one_hot((sel_b, rows), iota((sel_b, rows), 1) == RATE_B * iota((sel_b, rows), 0) + r)
    for r in range(RATE_B):
        pmt[:, r * sel_b : (r + 1) * sel_b] = one_hot(
            (rows, sel_b), iota((rows, sel_b), 0) == RATE_B * iota((rows, sel_b), 1) + r
        )
    table = jnp.zeros((heads, 128), jnp.int32)
    for h in range(heads):
        b = offs_b[z, h]
        c = late_other(b, offs_c[0, h])
        pair = jnp.where(iota((heads, 128), 1) == 0, b, c)
        table = jnp.where(iota((heads, 128), 0) == h, pair, table)
    ost[...] = table
    own_table = pltpu.make_async_copy(ost, osm.at[0], os_s.at[0])
    own_table.start()

    pl.semaphore_wait(barrier, (heads - 1) + (nz - 1) + 3)

    def mate_copy(n, device):
        src = (k_hbm, v_hbm)[n]
        return remote(src, mkv.at[n], mate_ss.at[n], mate_rs.at[n], device)

    @pl.when(core == 0)
    def _():
        for n in range(2):
            mate_copy(n, plane(i + 1)).start()

    def table_copy(d):
        return remote(ost, orc.at[d - 1], of_ss.at[d - 1], of_rs.at[d - 1], {"head": (y + d) % ny})

    for d in range(1, 4):
        table_copy(d).start()

    for copy in loads[:3]:
        copy.wait()

    def p1c(j, src):
        return remote(st1c.at[j], rc1c.at[src], p1c_ss.at[j], p1c_rs.at[src], plane(j))

    def p1b(j, src):
        return remote(st1b.at[j], rc1b.at[src], p1b_ss.at[j], p1b_rs.at[src], plane(j))

    def pick(d, _):
        j = (i + 1 + d) % heads
        b = offs_b[z, j]
        c = offs_c[0, j]
        cols = pl.ds(pl.multiple_of(j * HEAD_DIM, HEAD_DIM), HEAD_DIM)
        shape = (sel_b + sel_c, rows)
        row = iota(shape, 0)
        at = jnp.where(row < sel_b, RATE_B * row + b, top_stride * (row - sel_b) + c)
        chosen = one_hot(shape, iota(shape, 1) == at)
        for n, field in enumerate((qv, kv, vv)):
            found = dot(chosen, field[:, cols]).astype(BF16)
            st1b[j, :, n * HEAD_DIM : (n + 1) * HEAD_DIM] = found[:sel_b]
            st1c[j, :, n * HEAD_DIM : (n + 1) * HEAD_DIM] = found[sel_b:]

        @pl.when(j != i)
        def _():
            p1c(j, i).start()

        return 0

    lax.fori_loop(0, heads, pick, 0)

    def send_b(d, _):
        p1b((i + d) % heads, i).start()
        return 0

    lax.fori_loop(1, heads, send_b, 0)
    rc1b[i] = st1b[i]
    rc1c[i] = st1c[i]

    def x_send(h, part, to_right):
        n = 0 if to_right else 1
        slot = 0 if to_right else 2
        device = {"head": right if to_right else left}
        return remote(xs.at[h, part], xr.at[slot, h, part], x_ss.at[n, h, part], x_rs.at[slot, h, part], device)

    def x_recv(slot, h, part):
        return remote(xs.at[h, part], xr.at[slot, h, part], f_ss.at[h, part], x_rs.at[slot, h, part], {"head": right})

    def x_forward(h, part, to_right):
        device = {"head": right if to_right else left}
        return remote(
            xr.at[0 if to_right else 2, h, part], xr.at[1, h, part], f_ss.at[h, part], x_rs.at[1, h, part], device
        )

    def forward(h, part):
        x_recv(0, h, part).wait_recv()
        x_recv(2, h, part).wait_recv()

        @pl.when(h % 2 == 0)
        def _():
            x_forward(h, part, True).start()

        @pl.when(h % 2 == 1)
        def _():
            x_forward(h, part, False).start()

    def attend(key_parts, value_parts, query):
        scores = []
        for keys, allowed in key_parts:
            part = dot(keys, query, NT) * scale
            scores.append(part if allowed is None else jnp.where(allowed, part, NEG))
        top = functools.reduce(jnp.maximum, [jnp.max(part, axis=0, keepdims=True) for part in scores])
        weights = [jnp.exp2(part - top) for part in scores]
        total = functools.reduce(jnp.add, [jnp.sum(part, axis=0, keepdims=True) for part in weights])
        numer = functools.reduce(
            jnp.add, [dot(values, part.astype(BF16), TN) for values, part in zip(value_parts, weights)]
        )
        return numer / total, top + jnp.log2(total)

    def lowest(h, with_mate):
        cols = pl.ds(pl.multiple_of(h * HEAD_DIM, HEAD_DIM), HEAD_DIM)
        causal = iota((half, half), 0) <= iota((half, half), 1)
        for n in range(2):
            key_parts = [(kv[n * half : (n + 1) * half, cols], causal)]
            value_parts = [vv[n * half : (n + 1) * half, cols]]
            if n:
                key_parts.append((kv[:half, cols], None))
                value_parts.append(vv[:half, cols])
            if with_mate:
                key_parts.append((mkv[0, :, cols], None))
                value_parts.append(mkv[1, :, cols])
            out, level = attend(key_parts, value_parts, qv[n * half : (n + 1) * half, cols])
            oa[h, :, n * half : (n + 1) * half] = out
            la[h, :, n * half : (n + 1) * half] = jnp.broadcast_to(level, (8, half))

    @pl.when(core == 1)
    def _():
        for n in range(2):
            mate_copy(n, plane(i - 1)).wait_recv()

    def zg(t, src):
        return remote(ckv.at[src], ckv.at[src], zg_ss.at[t], zg_rs.at[src], along_z(t))

    def lowest_level(h, _):
        @pl.when(core == 1)
        def _():
            lowest(h, True)

        @pl.when(core == 0)
        def _():
            lowest(h, False)

        b = offs_b[z, h]
        c = late_other(b, offs_c[0, h])
        zero_free = jnp.logical_and(b != 0, c != 0)
        one_free = jnp.logical_and(b != 1, c != 1)
        first = jnp.where(zero_free, 0, jnp.where(one_free, 1, 2))
        three_free = jnp.logical_and(b != 3, c != 3)
        two_free = jnp.logical_and(b != 2, c != 2)
        second = jnp.where(three_free, 3, jnp.where(two_free, 2, 1))
        here = oa[h].astype(BF16)
        xs[h, 0, :sel_b] = dot(pm[first], here, NT).astype(BF16)
        xs[h, 0, sel_b:] = dot(pm[second], here, NT).astype(BF16)
        x_send(h, 0, True).start()
        x_send(h, 0, False).start()

        @pl.when(h == 3)
        def _():
            def wait_c(d, _):
                p1c(i, (i + d) % heads).wait_recv()
                return 0

            lax.fori_loop(1, heads, wait_c, 0)
            for j in range(heads):
                ckv[z, j * sel_c : (j + 1) * sel_c, :] = rc1c[j, :, HEAD_DIM:]

            def send_c(d, _):
                zg((z + d) % nz, z).start()
                return 0

            lax.fori_loop(1, nz, send_c, 0)

        return 0

    lax.fori_loop(0, heads, lowest_level, 0)

    def forward_early(h, _):
        forward(h, 0)
        return 0

    lax.fori_loop(0, heads // 2, forward_early, 0)

    def wait_b(d, _):
        p1b(i, (i + d) % heads).wait_recv()
        return 0

    lax.fori_loop(1, heads, wait_b, 0)

    def rb(j, src):
        return remote(rbst.at[j], rbrc.at[src], rb_ss.at[j], rb_rs.at[src], plane(j))

    def rc(j, src):
        return remote(rcst.at[j], rcrc.at[src], rc_ss.at[j], rc_rs.at[src], plane(j))

    def field_b(first, last, n):
        part = rc1b[first:last, :, n * HEAD_DIM : (n + 1) * HEAD_DIM]
        return part.reshape((last - first) * sel_b, HEAD_DIM)

    for pair in range(heads // 2):
        first = 2 * pair
        block = 2 * sel_b
        causal = iota((block, block), 0) <= iota((block, block), 1)
        key_parts = [(field_b(first, first + 2, 1), causal)]
        value_parts = [field_b(first, first + 2, 2)]
        if pair:
            key_parts.append((field_b(0, first, 1), None))
            value_parts.append(field_b(0, first, 2))
        out, level = attend(key_parts, value_parts, field_b(first, first + 2, 0))
        stats = stat_rows(16, level)
        for n in range(2):
            cols = slice(n * sel_b, (n + 1) * sel_b)
            rbst[first + n, :HEAD_DIM] = out[:, cols].astype(BF16)
            rbst[first + n, HEAD_DIM:] = stats[:, cols].astype(BF16)

            @pl.when(first + n != i)
            def _():
                rb(first + n, i).start()

    rbrc[i] = rbst[i]

    lax.fori_loop(heads // 2, heads, forward_early, 0)

    def wait_z(d, _):
        zg(z, (z + d) % nz).wait_recv()
        return 0

    lax.fori_loop(1, nz, wait_z, 0)
    count_c = heads * sel_c
    keys_c = ckv[:, :, :HEAD_DIM].reshape(nz * count_c, HEAD_DIM)
    values_c = ckv[:, :, HEAD_DIM:].reshape(nz * count_c, HEAD_DIM)
    query_c = rc1c[:, :, :HEAD_DIM].reshape(count_c, HEAD_DIM)
    shape_c = (nz * count_c, count_c)
    allowed_c = iota(shape_c, 0) <= iota(shape_c, 1) + z * count_c
    out, level = attend([(keys_c, allowed_c)], [values_c], query_c)
    flat = jnp.concatenate([out.T, stat_rows(HEAD_DIM, level).T], axis=1).astype(BF16)
    rcst[...] = flat.reshape(heads, sel_c, 2 * HEAD_DIM)
    rcrc[i] = rcst[i]

    def send_rc(d, _):
        rc((i + d) % heads, i).start()
        return 0

    lax.fori_loop(1, heads, send_rc, 0)

    def combine(h, _):
        @pl.when(h != i)
        def _():
            rb(i, h).wait_recv()
            rc(i, h).wait_recv()

        b = offs_b[z, h]
        c = offs_c[0, h]
        put_b = one_hot((sel_b, rows), iota((sel_b, rows), 1) == RATE_B * iota((sel_b, rows), 0) + b)
        put_c = one_hot((sel_c, rows), iota((sel_c, rows), 1) == top_stride * iota((sel_c, rows), 0) + c)
        from_b = dot(rbrc[h], put_b)
        from_c = dot(rcrc[h], put_c, TN)

        def level_of(field):
            return jnp.sum(field[HEAD_DIM : HEAD_DIM + 8], axis=0, keepdims=True)

        column = iota((1, rows), 1)
        level_a = la[h, 0:1, :]
        level_b = jnp.where(lax.rem(column, RATE_B) == b, level_of(from_b), NEG)
        level_c = jnp.where(lax.rem(column, top_stride) == c, level_of(from_c), NEG)
        peak = jnp.maximum(level_a, jnp.maximum(level_b, level_c))
        factor_a = jnp.exp2(level_a - peak)
        factor_b = jnp.exp2(level_b - peak)
        factor_c = jnp.exp2(level_c - peak)
        share = 1.0 / (factor_a + factor_b + factor_c)
        whole = (
            (factor_a * share) * oa[h]
            + (factor_b * share) * from_b[:HEAD_DIM]
            + (factor_c * share) * from_c[:HEAD_DIM]
        ).astype(BF16)
        xs[h, 1, :sel_b] = dot(pm[b], whole, NT).astype(BF16)
        xs[h, 1, sel_b:] = dot(pm[late_other(b, c)], whole, NT).astype(BF16)
        x_send(h, 1, True).start()
        x_send(h, 1, False).start()
        return 0

    lax.fori_loop(0, heads, combine, 0)

    own_table.wait()
    for d in range(1, 4):
        table_copy(d).wait_recv()
    tables = [pltpu.make_async_copy(orc.at[d - 1], osm.at[d], os_s.at[d]) for d in range(1, 4)]
    for copy in tables:
        copy.start()
    for copy in tables:
        copy.wait()
    loads[3].wait()

    def place(d, h, early, late):
        b = osm[d, h, 0]
        c = osm[d, h, 1]
        blocks = (early[:sel_b], early[sel_b:], late[:sel_b], late[sel_b:])
        cols = pl.ds(pl.multiple_of(h * HEAD_DIM, HEAD_DIM), HEAD_DIM)
        for r in range(RATE_B):
            at = r - jnp.where(b < r, 1, 0) - jnp.where(c < r, 1, 0)
            mine = lax.select(at == 0, blocks[0], blocks[1])
            mine = lax.select(c == r, blocks[3], mine)
            mine = lax.select(b == r, blocks[2], mine)
            att[d, r * sel_b : (r + 1) * sel_b, cols] = mine

    def place_own(h, _):
        place(0, h, xs[h, 0], xs[h, 1])
        return 0

    lax.fori_loop(0, heads, place_own, 0)
    chunk = 256

    def project(d, first, count, fresh):
        group = (y + ny - d) % ny
        depth = count * HEAD_DIM
        at = pl.multiple_of(group * width + first * HEAD_DIM, HEAD_DIM)
        block = att[d, :, pl.ds(pl.multiple_of(first * HEAD_DIM, HEAD_DIM), depth)]

        def columns(n, _):
            cols = pl.ds(pl.multiple_of(n * chunk, chunk), chunk)
            part = dot(block, wv[pl.ds(at, depth), cols])
            if fresh:
                acc[:, cols] = part
            else:
                acc[:, cols] += part
            return 0

        lax.fori_loop(0, width // chunk, columns, 0)

    project(0, 0, heads, True)

    def opposite(p):
        for n in range(2):
            h = 2 * p + n
            x_recv(1, h, 0).wait_recv()
            x_recv(1, h, 1).wait_recv()
            place(2, h, xr[1, h, 0], xr[1, h, 1])
        project(2, 2 * p, 2, False)

    def remote_pair(p, _):
        for n in range(2):
            forward(2 * p + n, 1)
        for d in (1, 3):
            for n in range(2):
                h = 2 * p + n
                place(d, h, xr[d - 1, h, 0], xr[d - 1, h, 1])
            project(d, 2 * p, 2, False)

        @pl.when(p > 0)
        def _():
            opposite(p - 1)

        return 0

    lax.fori_loop(0, heads // 2, remote_pair, 0)
    opposite(heads // 2 - 1)

    def finish(n, _):
        cols = pl.ds(pl.multiple_of(n * chunk, chunk), chunk)
        outv[:, cols] = dot(pmt[...], acc[:, cols].astype(BF16)).astype(BF16)
        return 0

    lax.fori_loop(0, width // chunk, finish, 0)
    store = pltpu.make_async_copy(outv, out_hbm, out_s)
    store.start()

    @pl.when(core == 0)
    def _():
        for n in range(2):
            mate_copy(n, plane(i + 1)).wait_send()

    for d in range(1, 4):
        table_copy(d).wait_send()

    def sent_plane(d, _):
        j = (i + d) % heads
        p1c(j, i).wait_send()
        p1b(j, i).wait_send()
        rb(j, i).wait_send()
        rc(j, i).wait_send()
        return 0

    lax.fori_loop(1, heads, sent_plane, 0)

    def sent_z(d, _):
        zg((z + d) % nz, z).wait_send()
        return 0

    lax.fori_loop(1, nz, sent_z, 0)

    def sent_y(h, _):
        for part in range(2):
            x_send(h, part, True).wait_send()
            x_send(h, part, False).wait_send()
            x_forward(h, part, True).wait_send()
        return 0

    lax.fori_loop(0, heads, sent_y, 0)
    store.wait()


def shards(queries, keys, values, offsets_b, offsets_c, out_weight):
    rows, width = queries.shape
    depth, features = out_weight.shape
    heads = width // HEAD_DIM
    nz = lax.axis_size("seq") // heads
    ny = lax.axis_size("head")
    sel_b = rows // RATE_B
    sel_c = rows // (lax.axis_size("seq") // 2)
    three = 3 * HEAD_DIM
    dma = pltpu.SemaphoreType.DMA
    hbm = pl.BlockSpec(memory_space=pl.ANY)
    smem = pl.BlockSpec(memory_space=pltpu.SMEM)
    scratch = [
        pltpu.VMEM((rows, width), BF16),
        pltpu.VMEM((rows, width), BF16),
        pltpu.VMEM((rows, width), BF16),
        pltpu.VMEM((2, rows, width), BF16),
        pltpu.VMEM((depth, features), BF16),
        pltpu.VMEM((heads, sel_b, three), BF16),
        pltpu.VMEM((heads, sel_c, three), BF16),
        pltpu.VMEM((heads, sel_b, three), BF16),
        pltpu.VMEM((heads, sel_c, three), BF16),
        pltpu.VMEM((nz, heads * sel_c, 2 * HEAD_DIM), BF16),
        pltpu.VMEM((RATE_B, sel_b, rows), BF16),
        pltpu.VMEM((rows, rows), BF16),
        pltpu.VMEM((heads, HEAD_DIM, rows), F32),
        pltpu.VMEM((heads, 8, rows), F32),
        pltpu.VMEM((heads, HEAD_DIM + 16, sel_b), BF16),
        pltpu.VMEM((heads, HEAD_DIM + 16, sel_b), BF16),
        pltpu.VMEM((heads, sel_c, 2 * HEAD_DIM), BF16),
        pltpu.VMEM((heads, sel_c, 2 * HEAD_DIM), BF16),
        pltpu.VMEM((heads, 2, 2 * sel_b, HEAD_DIM), BF16),
        pltpu.VMEM((3, heads, 2, 2 * sel_b, HEAD_DIM), BF16),
        pltpu.VMEM((ny, rows, width), BF16),
        pltpu.VMEM((rows, features), F32),
        pltpu.VMEM((rows, features), BF16),
        pltpu.VMEM((heads, 128), jnp.int32),
        pltpu.VMEM((3, heads, 128), jnp.int32),
        pltpu.SMEM((ny, heads, 128), jnp.int32),
        dma((4,)),
        dma((2,)),
        dma((2,)),
        dma((heads,)),
        dma((heads,)),
        dma((heads,)),
        dma((heads,)),
        dma((nz,)),
        dma((nz,)),
        dma((heads,)),
        dma((heads,)),
        dma((heads,)),
        dma((heads,)),
        dma((2, heads, 2)),
        dma((3, heads, 2)),
        dma((heads, 2)),
        dma((3,)),
        dma((3,)),
        dma((ny,)),
        dma(()),
    ]
    return pl.pallas_call(
        kernel,
        out_shape=jax.ShapeDtypeStruct((rows, features), BF16),
        in_specs=[hbm, hbm, hbm, smem, smem, hbm],
        out_specs=hbm,
        scratch_shapes=scratch,
        compiler_params=pltpu.CompilerParams(
            collective_id=0, has_side_effects=True, vmem_limit_bytes=56 * 2**20
        ),
    )(queries, keys, values, offsets_b, offsets_c.reshape(1, heads), out_weight)


def solution(mesh):
    placed = (
        P("seq", "head"),
        P("seq", "head"),
        P("seq", "head"),
        P(None, "head"),
        P("head"),
        P(None, "head"),
    )
    return jax.shard_map(
        shards, mesh=mesh, in_specs=placed, out_specs=P("seq", "head"), check_vma=False
    )
```

```python
import functools

import jax
import jax.numpy as jnp
from jax import lax
from jax.experimental import pallas as pl
from jax.experimental.pallas import tpu as pltpu
from jax.sharding import PartitionSpec as P

HEAD_DIM = 128
RATE_B = 4
LOG2E = 1.4426950408889634
NEG = -1e30
MESH = pl.DeviceIdType.MESH
F32 = jnp.float32
BF16 = jnp.bfloat16
NN = (((1,), (0,)), ((), ()))
NT = (((1,), (1,)), ((), ()))
TN = (((0,), (0,)), ((), ()))


def dot(a, b, dims=NN):
    return lax.dot_general(a, b, dims, preferred_element_type=F32)


def iota(shape, axis):
    return lax.broadcasted_iota(jnp.int32, shape, axis)


def one_hot(shape, condition):
    return jnp.where(condition, jnp.ones(shape, F32), jnp.zeros(shape, F32)).astype(BF16)


def late_residues(b, c):
    last = lax.rem(c, RATE_B)
    return jnp.where(last == b, lax.rem(b + 1, RATE_B), b), last


def place_of(r, second, last):
    free = r - jnp.where(second < r, 1, 0) - jnp.where(last < r, 1, 0)
    return jnp.where(last == r, 3, jnp.where(second == r, 2, free))


def stat_rows(count, level):
    high = level.astype(BF16).astype(F32)
    rest = level - high
    mid = rest.astype(BF16).astype(F32)
    low = rest - mid
    row = iota((count, level.shape[1]), 0)
    zero = jnp.zeros((count, level.shape[1]), F32)
    return jnp.where(row == 0, high, jnp.where(row == 1, mid, jnp.where(row == 2, low, zero)))


def kernel(
    q_hbm, k_hbm, v_hbm, offs_b, offs_c, w_hbm, out_hbm,
    qv, kv, vv, mkv, wv, qp, qf, kf, vf, nat, st1b, st1c, rc1b, rc1c, ckv, oa, la,
    rbst, rbrc, rcst, rcrc, xs, from_left0, from_left1, across0, across1, from_right0, from_right1, att, acc, outv,
    ost, orc, osm,
    ld_s, mate_ss, mate_rs, p1c_ss, p1c_rs, p1b_ss, p1b_rs, zg_ss, zg_rs,
    rb_ss, rb_rs, rc_ss, rc_rs, x_ss, x_rs, f_ss, of_ss, of_rs, os_s, out_s, hello, plane_in, all_in,
):
    rows, width = qv.shape
    heads = width // HEAD_DIM
    half = rows // 2
    sel_b = rows // RATE_B
    sel_c = st1c.shape[1]
    top_stride = rows // sel_c
    scale = HEAD_DIM**-0.5 * LOG2E

    s = lax.axis_index("seq")
    y = lax.axis_index("head")
    ny = lax.axis_size("head")
    nz = lax.axis_size("seq") // heads
    z = s // heads
    i = s % heads
    core = s % 2
    right = (y + 1) % ny
    left = (y + ny - 1) % ny

    def plane(j):
        return {"seq": z * heads + j}

    def along_z(t):
        return {"seq": t * heads + i}

    def remote(src, dst, ssem, rsem, device):
        return pltpu.make_async_remote_copy(
            src_ref=src, dst_ref=dst, send_sem=ssem, recv_sem=rsem, device_id=device, device_id_type=MESH
        )

    chunk = 256
    loads = [
        pltpu.make_async_copy(src, dst, ld_s.at[n])
        for n, (src, dst) in enumerate(((q_hbm, qv), (k_hbm, kv), (v_hbm, vv), (w_hbm, wv)))
    ]
    for copy in loads[:3]:
        copy.start()

    barrier = pltpu.get_barrier_semaphore()
    greeter = i == 2 * y
    peers = (heads - 1) + (ny - 1)
    ckv[...] = jnp.zeros(ckv.shape, BF16)

    def greet_plane(d, _):
        j = (i + d) % heads

        @pl.when(jnp.logical_or(greeter, j != 2 * y))
        def _():
            pl.semaphore_signal(barrier, 1, device_id=plane(j), device_id_type=MESH)

        return 0

    def each_plane(condition, act):
        def step(t, _):
            pl.when(condition(t))(lambda: act(t))
            return 0

        lax.fori_loop(0, nz, step, 0)

    def each_group(act):
        for d in range(1, 4):
            act((y + d) % ny)

    def greet_group(other):
        @pl.when(jnp.logical_or(greeter, i != 2 * other))
        def _():
            pl.semaphore_signal(barrier, 1, device_id={"head": other}, device_id_type=MESH)

    each_group(greet_group)
    lax.fori_loop(1, heads, greet_plane, 0)

    @pl.when(greeter)
    def _():
        def up(t):
            pl.semaphore_signal(barrier, 1, device_id=along_z(t), device_id_type=MESH)

        each_plane(lambda t: t > z, up)

    table = jnp.zeros((heads, 128), jnp.int32)
    for h in range(heads):
        second, last = late_residues(offs_b[z, h], offs_c[0, h])
        pair = jnp.where(iota((heads, 128), 1) == 0, second, last)
        table = jnp.where(iota((heads, 128), 0) == h, pair, table)
    ost[...] = table
    own_table = pltpu.make_async_copy(ost, osm.at[0], os_s.at[0])
    own_table.start()

    for copy, field, wide in zip(loads, (qv, kv, vv), (qf, kf, vf)):
        copy.wait()
        for h in range(heads):
            wide[h] = field[:, h * HEAD_DIM : (h + 1) * HEAD_DIM].astype(F32)

    def pick(j, _):
        b = offs_b[z, j]
        c = offs_c[0, j]
        cols = pl.ds(pl.multiple_of(j * HEAD_DIM, HEAD_DIM), HEAD_DIM)
        for n, wide in enumerate((qf, kf, vf)):
            part = slice(n * HEAD_DIM, (n + 1) * HEAD_DIM)
            st1c[j, :, part] = wide[j, pl.ds(c, sel_c, stride=top_stride), :].astype(BF16)
            st1b[j, :, part] = wide[j, pl.ds(b, sel_b, stride=RATE_B), :].astype(BF16)
        for r in range(RATE_B):
            qp[r * sel_b : (r + 1) * sel_b, cols] = qf[j, pl.ds(r, sel_b, stride=RATE_B), :].astype(BF16)
        return 0

    lax.fori_loop(0, heads, pick, 0)

    @pl.when(jnp.logical_not(greeter))
    def _():
        pl.semaphore_wait(barrier, peers)
        pl.semaphore_signal(hello, 1, device_id=plane(2 * y), device_id_type=MESH)

        def say(other):
            @pl.when(i == 2 * other)
            def _():
                pl.semaphore_signal(hello, 1, device_id={"head": other}, device_id_type=MESH)

        each_group(say)

    @pl.when(greeter)
    def _():
        pl.semaphore_wait(hello, peers)

    def mate_copy(n, device):
        cols = pl.ds((n // 2) * chunk, chunk)
        src, dst = (kv, vv)[n % 2], mkv.at[n % 2]
        return remote(src.at[:, cols], dst.at[:, cols], mate_ss.at[n], mate_rs.at[n], device)

    mates = 2 * (width // chunk)

    def mate_start(first, last):
        @pl.when(core == 0)
        def _():
            for n in range(first, last):
                mate_copy(n, plane(i + 1)).start()

    mate_start(0, 2)

    def table_copy(d):
        return remote(ost, orc.at[d - 1], of_ss.at[d - 1], of_rs.at[d - 1], {"head": (y + d) % ny})

    def p1c(j, src):
        return remote(st1c.at[j], rc1c.at[src], p1c_ss.at[j], p1c_rs.at[src], plane(j))

    def p1b(j, src):
        return remote(st1b.at[j], rc1b.at[src], p1b_ss.at[j], p1b_rs.at[src], plane(j))

    def send_c(d, _):
        p1c((i + d) % heads, i).start()
        return 0

    def send_b(d, _):
        p1b((i + d) % heads, i).start()
        return 0

    lax.fori_loop(1, heads, send_c, 0)
    lax.fori_loop(1, heads, send_b, 0)
    mate_start(2, mates)
    for d in range(1, 4):
        table_copy(d).start()
    loads[3].start()
    rc1b[i] = st1b[i]
    rc1c[i] = st1c[i]

    landing = ((from_left0, from_left1), (across0, across1), (from_right0, from_right1))
    few = heads // 2

    def blocks(ref, h, part):
        return ref.at[h, pl.ds(0, 2)] if part == 0 else ref.at[h, pl.ds(part + 1, 1)]

    def x_copy(h, part, to_right, group):
        n, slot = (0, 0) if to_right else (1, 2)
        device = {"head": right if to_right else left}
        dst = blocks(landing[slot][group], h % few, part)
        return remote(blocks(xs, h, part), dst, x_ss.at[n, h, part], x_rs.at[slot, h, part], device)

    def x_send(h, part):
        for group in range(2):

            @pl.when(h // few == group)
            def _():
                x_copy(h, part, True, group).start()
                x_copy(h, part, False, group).start()

    def x_recv(slot, h, part, group):
        dst = blocks(landing[slot][group], h % few, part)
        return remote(blocks(xs, h, part), dst, f_ss.at[h, part], x_rs.at[slot, h, part], {"head": right})

    def x_forward(h, part, to_right, group):
        device = {"head": right if to_right else left}
        src = blocks(landing[0 if to_right else 2][group], h % few, part)
        dst = blocks(landing[1][group], h % few, part)
        return remote(src, dst, f_ss.at[h, part], x_rs.at[1, h, part], device)

    def forward(part, group):
        def step(n, _):
            h = group * few + n
            x_recv(0, h, part, group).wait_recv()
            x_recv(2, h, part, group).wait_recv()

            @pl.when(h % 2 == 0)
            def _():
                x_forward(h, part, True, group).start()

            @pl.when(h % 2 == 1)
            def _():
                x_forward(h, part, False, group).start()

            return 0

        lax.fori_loop(0, few, step, 0)

    def attend(key_parts, value_parts, query):
        scores = []
        for keys, allowed in key_parts:
            part = dot(keys, query, NT) * scale
            scores.append(part if allowed is None else jnp.where(allowed, part, NEG))
        top = functools.reduce(jnp.maximum, [jnp.max(part, axis=0, keepdims=True) for part in scores])
        weights = [jnp.exp2(part - top) for part in scores]
        total = functools.reduce(jnp.add, [jnp.sum(part, axis=0, keepdims=True) for part in weights])
        numer = functools.reduce(
            jnp.add, [dot(values, part.astype(BF16), TN) for values, part in zip(value_parts, weights)]
        )
        return numer / total, top + jnp.log2(total)

    def lowest(h, with_mate):
        cols = pl.ds(pl.multiple_of(h * HEAD_DIM, HEAD_DIM), HEAD_DIM)
        for n in range(2):
            column = iota((rows, half), 1)
            residue = jnp.where(column < sel_b, 2 * n, 2 * n + 1 - RATE_B * sel_b)
            causal = iota((rows, half), 0) <= RATE_B * column + residue
            key_parts = [(kv[:, cols], causal)]
            value_parts = [vv[:, cols]]
            if with_mate:
                key_parts.append((mkv[0, :, cols], None))
                value_parts.append(mkv[1, :, cols])
            out, level = attend(key_parts, value_parts, qp[n * half : (n + 1) * half, cols])
            for t in range(2):
                part = slice(t * sel_b, (t + 1) * sel_b)
                oa[h, 2 * n + t] = out[:, part]
                la[h, 2 * n + t] = jnp.broadcast_to(level[:, part], (8, sel_b))

    def zg(t, src):
        return remote(ckv.at[src], ckv.at[src], zg_ss.at[t], zg_rs.at[src], along_z(t))

    def lowest_level(h, _):
        @pl.when(core == 1)
        def _():
            for n in range(mates // 2):

                @pl.when(h == n * (chunk // HEAD_DIM))
                def _():
                    for m in range(2):
                        mate_copy(2 * n + m, plane(i - 1)).wait_recv()

            lowest(h, True)

        @pl.when(core == 0)
        def _():
            lowest(h, False)

        second, last = late_residues(offs_b[z, h], offs_c[0, h])
        zero_free = jnp.logical_and(second != 0, last != 0)
        one_free = jnp.logical_and(second != 1, last != 1)
        three_free = jnp.logical_and(second != 3, last != 3)
        two_free = jnp.logical_and(second != 2, last != 2)
        xs[h, 0] = oa[h, jnp.where(zero_free, 0, jnp.where(one_free, 1, 2))].T.astype(BF16)
        xs[h, 1] = oa[h, jnp.where(three_free, 3, jnp.where(two_free, 2, 1))].T.astype(BF16)
        x_send(h, 0)

        @pl.when(jnp.logical_and(h == 0, jnp.logical_and(greeter, z > 0)))
        def _():
            pl.semaphore_wait(barrier, z)

            def down(t):
                pl.semaphore_signal(plane_in, 1, device_id=along_z(t), device_id_type=MESH)

            each_plane(lambda t: t < z, down)

        @pl.when(jnp.logical_and(h == 4, greeter))
        def _():
            @pl.when(z < nz - 1)
            def _():
                pl.semaphore_wait(plane_in, nz - 1 - z)

            def tell(d, _):
                pl.semaphore_signal(all_in, 1, device_id=plane((i + d) % heads), device_id_type=MESH)
                return 0

            lax.fori_loop(1, heads, tell, 0)

        @pl.when(h == 5)
        def _():
            def wait_c(d, _):
                p1c(i, (i + d) % heads).wait_recv()
                return 0

            lax.fori_loop(1, heads, wait_c, 0)
            for j in range(heads):
                ckv[z, j * sel_c : (j + 1) * sel_c, :] = rc1c[j, :, HEAD_DIM:]

            @pl.when(jnp.logical_not(greeter))
            def _():
                pl.semaphore_wait(all_in, 1)

            each_plane(lambda t: t > z, lambda t: zg(t, z).start())

        return 0

    lax.fori_loop(0, heads, lowest_level, 0)

    forward(0, 0)

    def wait_b(d, _):
        p1b(i, (i + d) % heads).wait_recv()
        return 0

    lax.fori_loop(1, heads, wait_b, 0)

    def rb(j, src):
        return remote(rbst.at[j], rbrc.at[src], rb_ss.at[j], rb_rs.at[src], plane(j))

    def rc(j, src):
        return remote(rcst.at[j], rcrc.at[src], rc_ss.at[j], rc_rs.at[src], plane(j))

    def field_b(first, last, n):
        part = rc1b[first:last, :, n * HEAD_DIM : (n + 1) * HEAD_DIM]
        return part.reshape((last - first) * sel_b, HEAD_DIM)

    for pair in range(heads // 2):
        first = 2 * pair
        block = 2 * sel_b
        causal = iota((block, block), 0) <= iota((block, block), 1)
        key_parts = [(field_b(first, first + 2, 1), causal)]
        value_parts = [field_b(first, first + 2, 2)]
        if pair:
            key_parts.append((field_b(0, first, 1), None))
            value_parts.append(field_b(0, first, 2))
        out, level = attend(key_parts, value_parts, field_b(first, first + 2, 0))
        stats = stat_rows(16, level)
        for n in range(2):
            cols = slice(n * sel_b, (n + 1) * sel_b)
            rbst[first + n, :HEAD_DIM] = out[:, cols].astype(BF16)
            rbst[first + n, HEAD_DIM:] = stats[:, cols].astype(BF16)

            @pl.when(first + n != i)
            def _():
                rb(first + n, i).start()

    rbrc[i] = rbst[i]

    forward(0, 1)

    def level_of(field):
        return jnp.sum(field[HEAD_DIM : HEAD_DIM + 8].astype(F32), axis=0, keepdims=True)

    def merge(h, residue, others):
        level_a = la[h, residue][0:1]
        peak = functools.reduce(jnp.maximum, [level for _, level in others], level_a)
        factor = jnp.exp2(level_a - peak)
        numer = factor * oa[h, residue]
        denom = factor
        for field, level in others:
            factor = jnp.exp2(level - peak)
            numer = numer + factor * field
            denom = denom + factor
        return (numer / denom).T.astype(BF16)

    def merge_second(h, _):
        @pl.when(h != i)
        def _():
            rb(i, h).wait_recv()

        b = offs_b[z, h]
        second, _ = late_residues(b, offs_c[0, h])
        level_b = jnp.where(second == b, level_of(rbrc[h]), NEG)
        xs[h, 2] = merge(h, second, [(rbrc[h, :HEAD_DIM].astype(F32), level_b)])
        x_send(h, 1)
        return 0

    lax.fori_loop(0, heads, merge_second, 0)

    each_plane(lambda t: t < z, lambda t: zg(z, t).wait_recv())
    count_c = heads * sel_c
    keys_c = ckv[:, :, :HEAD_DIM].reshape(nz * count_c, HEAD_DIM)
    values_c = ckv[:, :, HEAD_DIM:].reshape(nz * count_c, HEAD_DIM)
    query_c = rc1c[:, :, :HEAD_DIM].reshape(count_c, HEAD_DIM)
    shape_c = (nz * count_c, count_c)
    allowed_c = iota(shape_c, 0) <= iota(shape_c, 1) + z * count_c
    out, level = attend([(keys_c, allowed_c)], [values_c], query_c)
    flat = jnp.concatenate([out.T, stat_rows(HEAD_DIM, level).T], axis=1).astype(BF16)
    rcst[...] = flat.reshape(heads, sel_c, 2 * HEAD_DIM)
    rcrc[i] = rcst[i]

    def send_rc(d, _):
        rc((i + d) % heads, i).start()
        return 0

    lax.fori_loop(1, heads, send_rc, 0)

    forward(1, 0)

    def merge_last(h, _):
        @pl.when(h != i)
        def _():
            rc(i, h).wait_recv()

        b = offs_b[z, h]
        c = offs_c[0, h]
        _, last = late_residues(b, c)
        spot = lax.div(c, RATE_B)
        apart = top_stride // RATE_B
        put = one_hot((sel_c, sel_b), iota((sel_c, sel_b), 1) == apart * iota((sel_c, sel_b), 0) + spot)
        from_c = dot(rcrc[h], put, TN)
        level_b = jnp.where(last == b, level_of(rbrc[h]), NEG)
        level_c = jnp.where(lax.rem(iota((1, sel_b), 1), apart) == spot, level_of(from_c), NEG)
        xs[h, 3] = merge(h, last, [(rbrc[h, :HEAD_DIM].astype(F32), level_b), (from_c[:HEAD_DIM], level_c)])
        x_send(h, 2)
        return 0

    lax.fori_loop(0, heads, merge_last, 0)
    forward(1, 1)

    own_table.wait()
    for d in range(1, 4):
        table_copy(d).wait_recv()
    tables = [pltpu.make_async_copy(orc.at[d - 1], osm.at[d], os_s.at[d]) for d in range(1, 4)]
    for copy in tables:
        copy.start()
    for copy in tables:
        copy.wait()
    loads[3].wait()

    def store(n):
        cols = pl.ds(pl.multiple_of(n * chunk, chunk), chunk)
        return pltpu.make_async_copy(outv.at[:, cols], out_hbm.at[:, cols], out_s.at[n])

    def project(d, ref, first, count, fresh, final=False):
        def place(n, _):
            h = first + n
            cols = pl.ds(pl.multiple_of(h * HEAD_DIM, HEAD_DIM), HEAD_DIM)
            for r in range(RATE_B):
                att[d, r * sel_b : (r + 1) * sel_b, cols] = ref[n, place_of(r, osm[d, h, 0], osm[d, h, 1])]
            return 0

        lax.fori_loop(0, count, place, 0)
        group = (y + ny - d) % ny
        depth = count * HEAD_DIM
        at = pl.multiple_of(group * width + first * HEAD_DIM, HEAD_DIM)

        def columns(n, _):
            cols = pl.ds(pl.multiple_of(n * chunk, chunk), chunk)
            part = dot(att[d, :, first * HEAD_DIM : first * HEAD_DIM + depth], wv[pl.ds(at, depth), cols])
            if fresh:
                acc[:, cols] = part
            elif final:
                total = acc[:, cols] + part
                for t in range(chunk // 128):
                    for r in range(RATE_B):
                        block = total[r * sel_b : (r + 1) * sel_b, t * 128 : (t + 1) * 128]
                        nat[n, t, pl.ds(r, sel_b, stride=RATE_B), :] = block
                outv[:, cols] = jnp.concatenate([nat[n, t] for t in range(chunk // 128)], axis=1).astype(BF16)
                store(n).start()
            else:
                acc[:, cols] += part
            return 0

        lax.fori_loop(0, width // chunk, columns, 0)

    project(0, xs, 0, heads, True)
    for group in range(2):
        forward(2, group)
        project(1, from_left0 if group == 0 else from_left1, group * few, few, False)
        project(3, from_right0 if group == 0 else from_right1, group * few, few, False)
    @pl.when(core == 0)
    def _():
        for n in range(mates):
            mate_copy(n, plane(i + 1)).wait_send()

    for d in range(1, 4):
        table_copy(d).wait_send()

    def sent_plane(d, _):
        j = (i + d) % heads
        p1c(j, i).wait_send()
        p1b(j, i).wait_send()
        rb(j, i).wait_send()
        rc(j, i).wait_send()
        return 0

    lax.fori_loop(1, heads, sent_plane, 0)

    each_plane(lambda t: t > z, lambda t: zg(t, z).wait_send())

    def sent_y(h, _):
        for part in range(3):
            x_copy(h, part, True, 0).wait_send()
            x_copy(h, part, False, 0).wait_send()
            x_forward(h, part, True, 0).wait_send()
        return 0

    for group in range(2):

        def arrived(n, _):
            for part in range(3):
                x_recv(1, group * few + n, part, group).wait_recv()
            return 0

        lax.fori_loop(0, few, arrived, 0)
        if group == 1:
            lax.fori_loop(0, heads, sent_y, 0)
        project(2, landing[1][group], group * few, few, False, group == 1)

    for n in range(width // chunk):
        store(n).wait()


def shards(queries, keys, values, offsets_b, offsets_c, out_weight):
    rows, width = queries.shape
    depth, features = out_weight.shape
    heads = width // HEAD_DIM
    nz = lax.axis_size("seq") // heads
    ny = lax.axis_size("head")
    sel_b = rows // RATE_B
    sel_c = rows // (lax.axis_size("seq") // 2)
    three = 3 * HEAD_DIM
    dma = pltpu.SemaphoreType.DMA
    hbm = pl.BlockSpec(memory_space=pl.ANY)
    smem = pl.BlockSpec(memory_space=pltpu.SMEM)
    scratch = [
        pltpu.VMEM((rows, width), BF16),
        pltpu.VMEM((rows, width), BF16),
        pltpu.VMEM((rows, width), BF16),
        pltpu.VMEM((2, rows, width), BF16),
        pltpu.VMEM((depth, features), BF16),
        pltpu.VMEM((rows, width), BF16),
        *[pltpu.VMEM((heads, rows, HEAD_DIM), F32) for _ in range(3)],
        pltpu.VMEM((features // 256, 2, rows, 128), F32),
        pltpu.VMEM((heads, sel_b, three), BF16),
        pltpu.VMEM((heads, sel_c, three), BF16),
        pltpu.VMEM((heads, sel_b, three), BF16),
        pltpu.VMEM((heads, sel_c, three), BF16),
        pltpu.VMEM((nz, heads * sel_c, 2 * HEAD_DIM), BF16),
        pltpu.VMEM((heads, RATE_B, HEAD_DIM, sel_b), F32),
        pltpu.VMEM((heads, RATE_B, 8, sel_b), F32),
        pltpu.VMEM((heads, HEAD_DIM + 16, sel_b), BF16),
        pltpu.VMEM((heads, HEAD_DIM + 16, sel_b), BF16),
        pltpu.VMEM((heads, sel_c, 2 * HEAD_DIM), BF16),
        pltpu.VMEM((heads, sel_c, 2 * HEAD_DIM), BF16),
        pltpu.VMEM((heads, RATE_B, sel_b, HEAD_DIM), BF16),
        *[pltpu.VMEM((heads // 2, RATE_B, sel_b, HEAD_DIM), BF16) for _ in range(6)],
        pltpu.VMEM((ny, rows, width), BF16),
        pltpu.VMEM((rows, features), F32),
        pltpu.VMEM((rows, features), BF16),
        pltpu.VMEM((heads, 128), jnp.int32),
        pltpu.VMEM((3, heads, 128), jnp.int32),
        pltpu.SMEM((ny, heads, 128), jnp.int32),
        dma((4,)),
        dma((2 * (width // 256),)),
        dma((2 * (width // 256),)),
        dma((heads,)),
        dma((heads,)),
        dma((heads,)),
        dma((heads,)),
        dma((nz,)),
        dma((nz,)),
        dma((heads,)),
        dma((heads,)),
        dma((heads,)),
        dma((heads,)),
        dma((2, heads, 3)),
        dma((3, heads, 3)),
        dma((heads, 3)),
        dma((3,)),
        dma((3,)),
        dma((ny,)),
        dma((features // 256,)),
        *[pltpu.SemaphoreType.REGULAR for _ in range(3)],
    ]
    return pl.pallas_call(
        kernel,
        out_shape=jax.ShapeDtypeStruct((rows, features), BF16),
        in_specs=[hbm, hbm, hbm, smem, smem, hbm],
        out_specs=hbm,
        scratch_shapes=scratch,
        compiler_params=pltpu.CompilerParams(
            collective_id=0, has_side_effects=True, vmem_limit_bytes=56 * 2**20
        ),
    )(queries, keys, values, offsets_b, offsets_c.reshape(1, heads), out_weight)


def solution(mesh):
    placed = (
        P("seq", "head"),
        P("seq", "head"),
        P("seq", "head"),
        P(None, "head"),
        P("head"),
        P(None, "head"),
    )
    return jax.shard_map(
        shards, mesh=mesh, in_specs=placed, out_specs=P("seq", "head"), check_vma=False
    )
```

```python
import functools

import jax
import jax.numpy as jnp
from jax import lax
from jax.experimental import pallas as pl
from jax.experimental.pallas import tpu as pltpu
from jax.sharding import PartitionSpec as P

HEAD_DIM = 128
RATE_B = 4
LOG2E = 1.4426950408889634
NEG = -1e30
MESH = pl.DeviceIdType.MESH
F32 = jnp.float32
BF16 = jnp.bfloat16
NN = (((1,), (0,)), ((), ()))
NT = (((1,), (1,)), ((), ()))
TN = (((0,), (0,)), ((), ()))


def dot(a, b, dims=NN):
    return lax.dot_general(a, b, dims, preferred_element_type=F32)


def iota(shape, axis):
    return lax.broadcasted_iota(jnp.int32, shape, axis)


def one_hot(shape, condition):
    return jnp.where(condition, jnp.ones(shape, F32), jnp.zeros(shape, F32)).astype(BF16)


def late_residues(b, c):
    last = lax.rem(c, RATE_B)
    return jnp.where(last == b, lax.rem(b + 1, RATE_B), b), last


def place_of(r, second, last):
    free = r - jnp.where(second < r, 1, 0) - jnp.where(last < r, 1, 0)
    return jnp.where(last == r, 3, jnp.where(second == r, 2, free))


def stat_rows(count, level):
    high = level.astype(BF16).astype(F32)
    rest = level - high
    mid = rest.astype(BF16).astype(F32)
    low = rest - mid
    row = iota((count, level.shape[1]), 0)
    zero = jnp.zeros((count, level.shape[1]), F32)
    return jnp.where(row == 0, high, jnp.where(row == 1, mid, jnp.where(row == 2, low, zero)))


def kernel(
    q_hbm, k_hbm, v_hbm, offs_b, offs_c, w_hbm, out,
    qv, kv, vv, mkv, wv, qp, qf, kf, vf, nat, st1b, st1c, rc1b, rc1c, ckv, oa, la,
    rbst, rbrc, rcst, rcrc, xs, from_left0, from_left1, across0, across1, from_right0, from_right1, att, acc,
    ost, orc, osm,
    ld_s, mate_ss, mate_rs, p1c_ss, p1c_rs, p1b_ss, p1b_rs, zg_ss, zg_rs,
    rb_ss, rb_rs, rc_ss, rc_rs, x_ss, x_rs, f_ss, of_ss, of_rs, os_s, hello, plane_in, all_in,
):
    rows, width = qv.shape
    heads = width // HEAD_DIM
    half = rows // 2
    sel_b = rows // RATE_B
    sel_c = st1c.shape[1]
    top_stride = rows // sel_c
    scale = HEAD_DIM**-0.5 * LOG2E

    s = lax.axis_index("seq")
    y = lax.axis_index("head")
    ny = lax.axis_size("head")
    nz = lax.axis_size("seq") // heads
    z = s // heads
    i = s % heads
    core = s % 2
    right = (y + 1) % ny
    left = (y + ny - 1) % ny

    def plane(j):
        return {"seq": z * heads + j}

    def along_z(t):
        return {"seq": t * heads + i}

    def remote(src, dst, ssem, rsem, device):
        return pltpu.make_async_remote_copy(
            src_ref=src, dst_ref=dst, send_sem=ssem, recv_sem=rsem, device_id=device, device_id_type=MESH
        )

    chunk = 256
    loads = [
        pltpu.make_async_copy(src, dst, ld_s.at[n])
        for n, (src, dst) in enumerate(((q_hbm, qv), (k_hbm, kv), (v_hbm, vv), (w_hbm, wv)))
    ]
    for copy in loads[:3]:
        copy.start()

    barrier = pltpu.get_barrier_semaphore()
    greeter = i == 2 * y
    peers = (heads - 1) + (ny - 1)
    ckv[...] = jnp.zeros(ckv.shape, BF16)

    def greet_plane(d, _):
        j = (i + d) % heads

        @pl.when(jnp.logical_or(greeter, j != 2 * y))
        def _():
            pl.semaphore_signal(barrier, 1, device_id=plane(j), device_id_type=MESH)

        return 0

    def each_plane(condition, act):
        def step(t, _):
            pl.when(condition(t))(lambda: act(t))
            return 0

        lax.fori_loop(0, nz, step, 0)

    def each_group(act):
        for d in range(1, 4):
            act((y + d) % ny)

    def greet_group(other):
        @pl.when(jnp.logical_or(greeter, i != 2 * other))
        def _():
            pl.semaphore_signal(barrier, 1, device_id={"head": other}, device_id_type=MESH)

    each_group(greet_group)
    lax.fori_loop(1, heads, greet_plane, 0)

    @pl.when(greeter)
    def _():
        def up(t):
            pl.semaphore_signal(barrier, 1, device_id=along_z(t), device_id_type=MESH)

        each_plane(lambda t: t > z, up)

    table = jnp.zeros((heads, 128), jnp.int32)
    for h in range(heads):
        second, last = late_residues(offs_b[z, h], offs_c[0, h])
        pair = jnp.where(iota((heads, 128), 1) == 0, second, last)
        table = jnp.where(iota((heads, 128), 0) == h, pair, table)
    ost[...] = table
    own_table = pltpu.make_async_copy(ost, osm.at[0], os_s.at[0])
    own_table.start()

    for copy, field, wide in zip(loads, (qv, kv, vv), (qf, kf, vf)):
        copy.wait()
        for h in range(heads):
            wide[h] = field[:, h * HEAD_DIM : (h + 1) * HEAD_DIM].astype(F32)

    def pick(j, _):
        b = offs_b[z, j]
        c = offs_c[0, j]
        cols = pl.ds(pl.multiple_of(j * HEAD_DIM, HEAD_DIM), HEAD_DIM)
        for n, wide in enumerate((qf, kf, vf)):
            part = slice(n * HEAD_DIM, (n + 1) * HEAD_DIM)
            st1c[j, :, part] = wide[j, pl.ds(c, sel_c, stride=top_stride), :].astype(BF16)
            st1b[j, :, part] = wide[j, pl.ds(b, sel_b, stride=RATE_B), :].astype(BF16)
        for r in range(RATE_B):
            qp[r * sel_b : (r + 1) * sel_b, cols] = qf[j, pl.ds(r, sel_b, stride=RATE_B), :].astype(BF16)
        return 0

    lax.fori_loop(0, heads, pick, 0)

    @pl.when(jnp.logical_not(greeter))
    def _():
        pl.semaphore_wait(barrier, peers)
        pl.semaphore_signal(hello, 1, device_id=plane(2 * y), device_id_type=MESH)

        def say(other):
            @pl.when(i == 2 * other)
            def _():
                pl.semaphore_signal(hello, 1, device_id={"head": other}, device_id_type=MESH)

        each_group(say)

    @pl.when(greeter)
    def _():
        pl.semaphore_wait(hello, peers)

    def mate_copy(n, device):
        cols = pl.ds((n // 2) * chunk, chunk)
        src, dst = (kv, vv)[n % 2], mkv.at[n % 2]
        return remote(src.at[:, cols], dst.at[:, cols], mate_ss.at[n], mate_rs.at[n], device)

    mates = 2 * (width // chunk)

    def mate_start(first, last):
        @pl.when(core == 0)
        def _():
            for n in range(first, last):
                mate_copy(n, plane(i + 1)).start()

    mate_start(0, 2)

    def table_copy(d):
        return remote(ost, orc.at[d - 1], of_ss.at[d - 1], of_rs.at[d - 1], {"head": (y + d) % ny})

    def p1c(j, src):
        return remote(st1c.at[j], rc1c.at[src], p1c_ss.at[j], p1c_rs.at[src], plane(j))

    def p1b(j, src):
        return remote(st1b.at[j], rc1b.at[src], p1b_ss.at[j], p1b_rs.at[src], plane(j))

    def send_c(d, _):
        p1c((i + d) % heads, i).start()
        return 0

    def send_b(d, _):
        p1b((i + d) % heads, i).start()
        return 0

    lax.fori_loop(1, heads, send_c, 0)
    lax.fori_loop(1, heads, send_b, 0)
    mate_start(2, mates)
    for d in range(1, 4):
        table_copy(d).start()
    loads[3].start()
    rc1b[i] = st1b[i]
    rc1c[i] = st1c[i]

    landing = ((from_left0, from_left1), (across0, across1), (from_right0, from_right1))
    few = heads // 2

    def units(part):
        return heads if part == 0 else few

    def blocks(ref, u, part):
        return ref.at[u, pl.ds(0, 2)] if part == 0 else ref.at[pl.ds(2 * u, 2), pl.ds(part + 1, 1)]

    def landed(slot, u, part, group):
        return blocks(landing[slot][group], u % (units(part) // 2), part)

    def x_copy(u, part, to_right, group):
        n, slot = (0, 0) if to_right else (1, 2)
        device = {"head": right if to_right else left}
        dst = landed(slot, u, part, group)
        return remote(blocks(xs, u, part), dst, x_ss.at[n, u, part], x_rs.at[slot, u, part], device)

    def x_send(u, part):
        for group in range(2):

            @pl.when(u // (units(part) // 2) == group)
            def _():
                x_copy(u, part, True, group).start()
                x_copy(u, part, False, group).start()

    def x_recv(slot, u, part, group):
        dst = landed(slot, u, part, group)
        return remote(blocks(xs, u, part), dst, f_ss.at[u, part], x_rs.at[slot, u, part], {"head": right})

    def x_forward(u, part, to_right, group):
        device = {"head": right if to_right else left}
        src = landed(0 if to_right else 2, u, part, group)
        dst = landed(1, u, part, group)
        return remote(src, dst, f_ss.at[u, part], x_rs.at[1, u, part], device)

    def each_unit(part, group, act):
        count = units(part) // 2

        def step(n, _):
            act(group * count + n)
            return 0

        lax.fori_loop(0, count, step, 0)

    def forward(part, group):
        def act(u):
            x_recv(0, u, part, group).wait_recv()
            x_recv(2, u, part, group).wait_recv()

            @pl.when(u % 2 == 0)
            def _():
                x_forward(u, part, True, group).start()

            @pl.when(u % 2 == 1)
            def _():
                x_forward(u, part, False, group).start()

        each_unit(part, group, act)

    def attend(key_parts, value_parts, query):
        scores = []
        for keys, allowed in key_parts:
            part = dot(keys, query, NT) * scale
            scores.append(part if allowed is None else jnp.where(allowed, part, NEG))
        top = functools.reduce(jnp.maximum, [jnp.max(part, axis=0, keepdims=True) for part in scores])
        weights = [jnp.exp2(part - top) for part in scores]
        total = functools.reduce(jnp.add, [jnp.sum(part, axis=0, keepdims=True) for part in weights])
        numer = functools.reduce(
            jnp.add, [dot(values, part.astype(BF16), TN) for values, part in zip(value_parts, weights)]
        )
        return numer * (1.0 / total), top + jnp.log2(total)

    def lowest(h, with_mate):
        cols = pl.ds(pl.multiple_of(h * HEAD_DIM, HEAD_DIM), HEAD_DIM)
        for n in range(2):
            column = iota((rows, half), 1)
            residue = jnp.where(column < sel_b, 2 * n, 2 * n + 1 - RATE_B * sel_b)
            causal = iota((rows, half), 0) <= RATE_B * column + residue
            key_parts = [(kv[:, cols], causal)]
            value_parts = [vv[:, cols]]
            if with_mate:
                key_parts.append((mkv[0, :, cols], None))
                value_parts.append(mkv[1, :, cols])
            result, level = attend(key_parts, value_parts, qp[n * half : (n + 1) * half, cols])
            for t in range(2):
                part = slice(t * sel_b, (t + 1) * sel_b)
                oa[h, 2 * n + t] = result[:, part]
                la[h, 2 * n + t] = jnp.broadcast_to(level[:, part], (8, sel_b))

    def zg(t, src):
        return remote(ckv.at[src], ckv.at[src], zg_ss.at[t], zg_rs.at[src], along_z(t))

    go_up = jnp.where(z < 2, 6, 5)

    def lowest_level(h, _):
        @pl.when(core == 1)
        def _():
            for n in range(mates // 2):

                @pl.when(h == n * (chunk // HEAD_DIM))
                def _():
                    for m in range(2):
                        mate_copy(2 * n + m, plane(i - 1)).wait_recv()

            lowest(h, True)

        @pl.when(core == 0)
        def _():
            lowest(h, False)

        second, last = late_residues(offs_b[z, h], offs_c[0, h])
        zero_free = jnp.logical_and(second != 0, last != 0)
        one_free = jnp.logical_and(second != 1, last != 1)
        three_free = jnp.logical_and(second != 3, last != 3)
        two_free = jnp.logical_and(second != 2, last != 2)
        xs[h, 0] = oa[h, jnp.where(zero_free, 0, jnp.where(one_free, 1, 2))].T.astype(BF16)
        xs[h, 1] = oa[h, jnp.where(three_free, 3, jnp.where(two_free, 2, 1))].T.astype(BF16)
        x_send(h, 0)

        @pl.when(jnp.logical_and(h == 0, jnp.logical_and(greeter, z > 0)))
        def _():
            pl.semaphore_wait(barrier, z)

            def down(t):
                pl.semaphore_signal(plane_in, 1, device_id=along_z(t), device_id_type=MESH)

            each_plane(lambda t: t < z, down)

        @pl.when(jnp.logical_and(h == go_up - 1, greeter))
        def _():
            @pl.when(z < nz - 1)
            def _():
                pl.semaphore_wait(plane_in, nz - 1 - z)

            def tell(d, _):
                pl.semaphore_signal(all_in, 1, device_id=plane((i + d) % heads), device_id_type=MESH)
                return 0

            lax.fori_loop(1, heads, tell, 0)

        @pl.when(h == go_up)
        def _():
            def wait_c(d, _):
                p1c(i, (i + d) % heads).wait_recv()
                return 0

            lax.fori_loop(1, heads, wait_c, 0)
            for j in range(heads):
                ckv[z, j * sel_c : (j + 1) * sel_c, :] = rc1c[j, :, HEAD_DIM:]

            @pl.when(jnp.logical_not(greeter))
            def _():
                pl.semaphore_wait(all_in, 1)

            each_plane(lambda t: t > z, lambda t: zg(t, z).start())

        return 0

    lax.fori_loop(0, heads, lowest_level, 0)


    forward(0, 0)

    def wait_b(d, _):
        p1b(i, (i + d) % heads).wait_recv()
        return 0

    lax.fori_loop(1, heads, wait_b, 0)

    def rb(j, src):
        return remote(rbst.at[j], rbrc.at[src], rb_ss.at[j], rb_rs.at[src], plane(j))

    def rc(j, src):
        return remote(rcst.at[j], rcrc.at[src], rc_ss.at[j], rc_rs.at[src], plane(j))

    def field_b(first, last, n):
        part = rc1b[first:last, :, n * HEAD_DIM : (n + 1) * HEAD_DIM]
        return part.reshape((last - first) * sel_b, HEAD_DIM)

    for pair in range(heads // 2):
        first = 2 * pair
        block = 2 * sel_b
        causal = iota((block, block), 0) <= iota((block, block), 1)
        key_parts = [(field_b(first, first + 2, 1), causal)]
        value_parts = [field_b(first, first + 2, 2)]
        if pair:
            key_parts.append((field_b(0, first, 1), None))
            value_parts.append(field_b(0, first, 2))
        result, level = attend(key_parts, value_parts, field_b(first, first + 2, 0))
        stats = stat_rows(16, level)
        for n in range(2):
            cols = slice(n * sel_b, (n + 1) * sel_b)
            rbst[first + n, :HEAD_DIM] = result[:, cols].astype(BF16)
            rbst[first + n, HEAD_DIM:] = stats[:, cols].astype(BF16)

            @pl.when(first + n != i)
            def _():
                rb(first + n, i).start()

    rbrc[i] = rbst[i]
    forward(0, 1)


    def level_of(field):
        return jnp.sum(field[HEAD_DIM : HEAD_DIM + 8].astype(F32), axis=0, keepdims=True)

    def merge(h, residue, others):
        level_a = la[h, residue][0:1]
        peak = functools.reduce(jnp.maximum, [level for _, level in others], level_a)
        factors = [jnp.exp2(level - peak) for level in [level_a] + [level for _, level in others]]
        share = 1.0 / functools.reduce(jnp.add, factors)
        numer = (factors[0] * share) * oa[h, residue]
        for (field, _), factor in zip(others, factors[1:]):
            numer = numer + (factor * share) * field
        return numer.T.astype(BF16)

    def merge_second(h, _):
        @pl.when(h != i)
        def _():
            rb(i, h).wait_recv()

        b = offs_b[z, h]
        second, _ = late_residues(b, offs_c[0, h])
        level_b = jnp.where(second == b, level_of(rbrc[h]), NEG)
        xs[h, 2] = merge(h, second, [(rbrc[h, :HEAD_DIM].astype(F32), level_b)])

        @pl.when(h % 2 == 1)
        def _():
            x_send(h // 2, 1)

        return 0

    lax.fori_loop(0, heads, merge_second, 0)

    each_plane(lambda t: t < z, lambda t: zg(z, t).wait_recv())
    count_c = heads * sel_c
    keys_c = ckv[:, :, :HEAD_DIM].reshape(nz * count_c, HEAD_DIM)
    values_c = ckv[:, :, HEAD_DIM:].reshape(nz * count_c, HEAD_DIM)
    query_c = rc1c[:, :, :HEAD_DIM].reshape(count_c, HEAD_DIM)
    shape_c = (nz * count_c, count_c)
    allowed_c = iota(shape_c, 0) <= iota(shape_c, 1) + z * count_c
    result, level = attend([(keys_c, allowed_c)], [values_c], query_c)
    flat = jnp.concatenate([result.T, stat_rows(HEAD_DIM, level).T], axis=1).astype(BF16)
    rcst[...] = flat.reshape(heads, sel_c, 2 * HEAD_DIM)
    rcrc[i] = rcst[i]

    def send_rc(d, _):
        rc((i + d) % heads, i).start()
        return 0

    lax.fori_loop(1, heads, send_rc, 0)


    def merge_last(h, _):
        @pl.when(h != i)
        def _():
            rc(i, h).wait_recv()

        b = offs_b[z, h]
        c = offs_c[0, h]
        _, last = late_residues(b, c)
        spot = lax.div(c, RATE_B)
        apart = top_stride // RATE_B
        put = one_hot((sel_c, sel_b), iota((sel_c, sel_b), 1) == apart * iota((sel_c, sel_b), 0) + spot)
        from_c = dot(rcrc[h], put, TN)
        level_b = jnp.where(last == b, level_of(rbrc[h]), NEG)
        level_c = jnp.where(lax.rem(iota((1, sel_b), 1), apart) == spot, level_of(from_c), NEG)
        xs[h, 3] = merge(h, last, [(rbrc[h, :HEAD_DIM].astype(F32), level_b), (from_c[:HEAD_DIM], level_c)])

        @pl.when(h % 2 == 1)
        def _():
            x_send(h // 2, 2)

        return 0

    lax.fori_loop(0, heads, merge_last, 0)
    forward(1, 0)
    forward(1, 1)

    own_table.wait()
    for d in range(1, 4):
        table_copy(d).wait_recv()
    tables = [pltpu.make_async_copy(orc.at[d - 1], osm.at[d], os_s.at[d]) for d in range(1, 4)]
    for copy in tables:
        copy.start()
    for copy in tables:
        copy.wait()
    loads[3].wait()

    def project(d, ref, first, count, fresh, final=False):
        def place(n, _):
            h = first + n
            cols = pl.ds(pl.multiple_of(h * HEAD_DIM, HEAD_DIM), HEAD_DIM)
            for r in range(RATE_B):
                att[d, r * sel_b : (r + 1) * sel_b, cols] = ref[n, place_of(r, osm[d, h, 0], osm[d, h, 1])]
            return 0

        lax.fori_loop(0, count, place, 0)
        group = (y + ny - d) % ny
        depth = count * HEAD_DIM
        at = pl.multiple_of(group * width + first * HEAD_DIM, HEAD_DIM)

        def columns(n, _):
            cols = pl.ds(pl.multiple_of(n * chunk, chunk), chunk)
            part = dot(att[d, :, first * HEAD_DIM : first * HEAD_DIM + depth], wv[pl.ds(at, depth), cols])
            if fresh:
                acc[:, cols] = part
            elif final:
                total = acc[:, cols] + part
                for t in range(chunk // 128):
                    for r in range(RATE_B):
                        block = total[r * sel_b : (r + 1) * sel_b, t * 128 : (t + 1) * 128]
                        nat[n, t, pl.ds(r, sel_b, stride=RATE_B), :] = block
                out[:, cols] = jnp.concatenate([nat[n, t] for t in range(chunk // 128)], axis=1).astype(BF16)
            else:
                acc[:, cols] += part
            return 0

        lax.fori_loop(0, width // chunk, columns, 0)

    project(0, xs, 0, heads, True)
    for group in range(2):
        forward(2, group)
        project(1, from_left0 if group == 0 else from_left1, group * few, few, False)
        project(3, from_right0 if group == 0 else from_right1, group * few, few, False)
    @pl.when(core == 0)
    def _():
        for n in range(mates):
            mate_copy(n, plane(i + 1)).wait_send()

    for d in range(1, 4):
        table_copy(d).wait_send()

    def sent_plane(d, _):
        j = (i + d) % heads
        p1c(j, i).wait_send()
        p1b(j, i).wait_send()
        rb(j, i).wait_send()
        rc(j, i).wait_send()
        return 0

    lax.fori_loop(1, heads, sent_plane, 0)

    each_plane(lambda t: t > z, lambda t: zg(t, z).wait_send())

    def sent_y(u, part):
        x_copy(u, part, True, 0).wait_send()
        x_copy(u, part, False, 0).wait_send()
        x_forward(u, part, True, 0).wait_send()

    for group in range(2):
        if group == 1:
            for part in range(3):
                for half_of in range(2):
                    each_unit(part, half_of, lambda u, part=part: sent_y(u, part))
        for part in range(3):
            each_unit(part, group, lambda u, part=part: x_recv(1, u, part, group).wait_recv())
        project(2, landing[1][group], group * few, few, False, group == 1)


def shards(queries, keys, values, offsets_b, offsets_c, out_weight):
    rows, width = queries.shape
    depth, features = out_weight.shape
    heads = width // HEAD_DIM
    nz = lax.axis_size("seq") // heads
    ny = lax.axis_size("head")
    sel_b = rows // RATE_B
    sel_c = rows // (lax.axis_size("seq") // 2)
    three = 3 * HEAD_DIM
    dma = pltpu.SemaphoreType.DMA
    hbm = pl.BlockSpec(memory_space=pl.ANY)
    smem = pl.BlockSpec(memory_space=pltpu.SMEM)
    scratch = [
        pltpu.VMEM((rows, width), BF16),
        pltpu.VMEM((rows, width), BF16),
        pltpu.VMEM((rows, width), BF16),
        pltpu.VMEM((2, rows, width), BF16),
        pltpu.VMEM((depth, features), BF16),
        pltpu.VMEM((rows, width), BF16),
        *[pltpu.VMEM((heads, rows, HEAD_DIM), F32) for _ in range(3)],
        pltpu.VMEM((features // 256, 2, rows, 128), F32),
        pltpu.VMEM((heads, sel_b, three), BF16),
        pltpu.VMEM((heads, sel_c, three), BF16),
        pltpu.VMEM((heads, sel_b, three), BF16),
        pltpu.VMEM((heads, sel_c, three), BF16),
        pltpu.VMEM((nz, heads * sel_c, 2 * HEAD_DIM), BF16),
        pltpu.VMEM((heads, RATE_B, HEAD_DIM, sel_b), F32),
        pltpu.VMEM((heads, RATE_B, 8, sel_b), F32),
        pltpu.VMEM((heads, HEAD_DIM + 16, sel_b), BF16),
        pltpu.VMEM((heads, HEAD_DIM + 16, sel_b), BF16),
        pltpu.VMEM((heads, sel_c, 2 * HEAD_DIM), BF16),
        pltpu.VMEM((heads, sel_c, 2 * HEAD_DIM), BF16),
        pltpu.VMEM((heads, RATE_B, sel_b, HEAD_DIM), BF16),
        *[pltpu.VMEM((heads // 2, RATE_B, sel_b, HEAD_DIM), BF16) for _ in range(6)],
        pltpu.VMEM((ny, rows, width), BF16),
        pltpu.VMEM((rows, features), F32),
        pltpu.VMEM((heads, 128), jnp.int32),
        pltpu.VMEM((3, heads, 128), jnp.int32),
        pltpu.SMEM((ny, heads, 128), jnp.int32),
        dma((4,)),
        dma((2 * (width // 256),)),
        dma((2 * (width // 256),)),
        dma((heads,)),
        dma((heads,)),
        dma((heads,)),
        dma((heads,)),
        dma((nz,)),
        dma((nz,)),
        dma((heads,)),
        dma((heads,)),
        dma((heads,)),
        dma((heads,)),
        dma((2, heads, 3)),
        dma((3, heads, 3)),
        dma((heads, 3)),
        dma((3,)),
        dma((3,)),
        dma((ny,)),
        *[pltpu.SemaphoreType.REGULAR for _ in range(3)],
    ]
    return pl.pallas_call(
        kernel,
        out_shape=jax.ShapeDtypeStruct((rows, features), BF16),
        in_specs=[hbm, hbm, hbm, smem, smem, hbm],
        out_specs=pl.BlockSpec(memory_space=pltpu.VMEM),
        scratch_shapes=scratch,
        compiler_params=pltpu.CompilerParams(
            collective_id=0, has_side_effects=True, vmem_limit_bytes=52 * 2**20
        ),
    )(queries, keys, values, offsets_b, offsets_c.reshape(1, heads), out_weight)


def solution(mesh):
    placed = (
        P("seq", "head"),
        P("seq", "head"),
        P("seq", "head"),
        P(None, "head"),
        P("head"),
        P(None, "head"),
    )
    return jax.shard_map(
        shards, mesh=mesh, in_specs=placed, out_specs=P("seq", "head"), check_vma=False
    )
```

```python
import functools

import jax
import jax.numpy as jnp
from jax import lax
from jax.experimental import pallas as pl
from jax.experimental.pallas import tpu as pltpu
from jax.sharding import PartitionSpec as P

HEAD_DIM = 128
RATE_B = 4
LOG2E = 1.4426950408889634
NEG = -1e30
MESH = pl.DeviceIdType.MESH
F32 = jnp.float32
BF16 = jnp.bfloat16
NN = (((1,), (0,)), ((), ()))
NT = (((1,), (1,)), ((), ()))
TN = (((0,), (0,)), ((), ()))


def dot(a, b, dims=NN):
    return lax.dot_general(a, b, dims, preferred_element_type=F32)


def iota(shape, axis):
    return lax.broadcasted_iota(jnp.int32, shape, axis)


def one_hot(shape, condition):
    return jnp.where(condition, jnp.ones(shape, F32), jnp.zeros(shape, F32)).astype(BF16)


def late_residues(b, c):
    last = lax.rem(c, RATE_B)
    return jnp.where(last == b, lax.rem(b + 1, RATE_B), b), last


def place_of(r, second, last):
    free = r - jnp.where(second < r, 1, 0) - jnp.where(last < r, 1, 0)
    return jnp.where(last == r, 3, jnp.where(second == r, 2, free))


def stat_rows(count, level):
    high = level.astype(BF16).astype(F32)
    rest = level - high
    mid = rest.astype(BF16).astype(F32)
    low = rest - mid
    row = iota((count, level.shape[1]), 0)
    zero = jnp.zeros((count, level.shape[1]), F32)
    return jnp.where(row == 0, high, jnp.where(row == 1, mid, jnp.where(row == 2, low, zero)))


def kernel(
    q_hbm, k_hbm, v_hbm, offs_b, offs_c, w_hbm, out,
    qv, kv, vv, mkv, wv, qp, qf, kf, vf, nat, st1b, st1c, rc1b, rc1c, ckv, oa, la,
    rbst, rbrc, rcst, rcrc, xs, from_left0, from_left1, across0, across1, from_right0, from_right1, att, acc,
    ost, orc, osm,
    ld_s, mate_ss, mate_rs, p1c_ss, p1c_rs, p1b_ss, p1b_rs, zg_ss, zg_rs,
    rb_ss, rb_rs, rc_ss, rc_rs, x_ss, x_rs, f_ss, of_ss, of_rs, os_s, hello, plane_in, all_in,
):
    rows, width = qv.shape
    heads = width // HEAD_DIM
    half = rows // 2
    sel_b = rows // RATE_B
    sel_c = st1c.shape[1]
    top_stride = rows // sel_c
    scale = HEAD_DIM**-0.5 * LOG2E

    s = lax.axis_index("seq")
    y = lax.axis_index("head")
    ny = lax.axis_size("head")
    nz = lax.axis_size("seq") // heads
    z = s // heads
    i = s % heads
    core = s % 2
    right = (y + 1) % ny
    left = (y + ny - 1) % ny

    def plane(j):
        return {"seq": z * heads + j}

    def along_z(t):
        return {"seq": t * heads + i}

    def remote(src, dst, ssem, rsem, device):
        return pltpu.make_async_remote_copy(
            src_ref=src, dst_ref=dst, send_sem=ssem, recv_sem=rsem, device_id=device, device_id_type=MESH
        )

    chunk = 256
    loads = [
        pltpu.make_async_copy(src, dst, ld_s.at[n])
        for n, (src, dst) in enumerate(((q_hbm, qv), (k_hbm, kv), (v_hbm, vv), (w_hbm, wv)))
    ]
    for copy in loads[:3]:
        copy.start()

    barrier = pltpu.get_barrier_semaphore()
    greeter = i == 2 * y
    peers = (heads - 1) + (ny - 1)
    ckv[...] = jnp.zeros(ckv.shape, BF16)

    def greet_plane(d, _):
        j = (i + d) % heads

        @pl.when(jnp.logical_or(greeter, j != 2 * y))
        def _():
            pl.semaphore_signal(barrier, 1, device_id=plane(j), device_id_type=MESH)

        return 0

    def each_plane(condition, act):
        def step(t, _):
            pl.when(condition(t))(lambda: act(t))
            return 0

        lax.fori_loop(0, nz, step, 0)

    def each_group(act):
        for d in range(1, 4):
            act((y + d) % ny)

    def greet_group(other):
        @pl.when(jnp.logical_or(greeter, i != 2 * other))
        def _():
            pl.semaphore_signal(barrier, 1, device_id={"head": other}, device_id_type=MESH)

    each_group(greet_group)
    lax.fori_loop(1, heads, greet_plane, 0)

    @pl.when(greeter)
    def _():
        def up(t):
            pl.semaphore_signal(barrier, 1, device_id=along_z(t), device_id_type=MESH)

        each_plane(lambda t: t > z, up)

    table = jnp.zeros((heads, 128), jnp.int32)
    for h in range(heads):
        second, last = late_residues(offs_b[z, h], offs_c[0, h])
        pair = jnp.where(iota((heads, 128), 1) == 0, second, last)
        table = jnp.where(iota((heads, 128), 0) == h, pair, table)
    ost[...] = table
    own_table = pltpu.make_async_copy(ost, osm.at[0], os_s.at[0])
    own_table.start()

    for copy, field, wide in zip(loads, (qv, kv, vv), (qf, kf, vf)):
        copy.wait()
        for h in range(heads):
            wide[h, :rows] = field[:, h * HEAD_DIM : (h + 1) * HEAD_DIM].astype(F32)

    def pick(j, _):
        b = offs_b[z, j]
        c = offs_c[0, j]
        cols = pl.ds(pl.multiple_of(j * HEAD_DIM, HEAD_DIM), HEAD_DIM)
        for n, wide in enumerate((qf, kf, vf)):
            part = slice(n * HEAD_DIM, (n + 1) * HEAD_DIM)
            st1c[j, :, part] = wide[j, pl.ds(c, sel_c, stride=top_stride), :].astype(BF16)
            st1b[j, :, part] = wide[j, pl.ds(b, sel_b, stride=RATE_B), :].astype(BF16)
        for r in range(RATE_B):
            qp[r * sel_b : (r + 1) * sel_b, cols] = qf[j, pl.ds(r, sel_b, stride=RATE_B), :].astype(BF16)
        return 0

    lax.fori_loop(0, heads, pick, 0)

    @pl.when(jnp.logical_not(greeter))
    def _():
        pl.semaphore_wait(barrier, peers)
        pl.semaphore_signal(hello, 1, device_id=plane(2 * y), device_id_type=MESH)

        def say(other):
            @pl.when(i == 2 * other)
            def _():
                pl.semaphore_signal(hello, 1, device_id={"head": other}, device_id_type=MESH)

        each_group(say)

    @pl.when(greeter)
    def _():
        pl.semaphore_wait(hello, peers)

    def mate_copy(n, device):
        cols = pl.ds((n // 2) * chunk, chunk)
        src, dst = (kv, vv)[n % 2], mkv.at[n % 2]
        return remote(src.at[:, cols], dst.at[:, cols], mate_ss.at[n], mate_rs.at[n], device)

    mates = 2 * (width // chunk)

    def mate_start(first, last):
        @pl.when(core == 0)
        def _():
            for n in range(first, last):
                mate_copy(n, plane(i + 1)).start()

    mate_start(0, 2)

    def table_copy(d):
        return remote(ost, orc.at[d - 1], of_ss.at[d - 1], of_rs.at[d - 1], {"head": (y + d) % ny})

    def p1c(j, src):
        return remote(st1c.at[j], rc1c.at[src], p1c_ss.at[j], p1c_rs.at[src], plane(j))

    def p1b(j, src):
        return remote(st1b.at[j], rc1b.at[src], p1b_ss.at[j], p1b_rs.at[src], plane(j))

    def send_c(d, _):
        p1c((i + d) % heads, i).start()
        return 0

    def send_b(d, _):
        p1b((i + d) % heads, i).start()
        return 0

    lax.fori_loop(1, heads, send_c, 0)
    lax.fori_loop(1, heads, send_b, 0)
    mate_start(2, mates)
    for d in range(1, 4):
        table_copy(d).start()
    loads[3].start()
    rc1b[i] = st1b[i]
    rc1c[i] = st1c[i]

    landing = ((from_left0, from_left1), (across0, across1), (from_right0, from_right1))
    few = heads // 2

    def units(part):
        return heads if part == 0 else few

    def blocks(ref, u, part):
        return ref.at[u, pl.ds(0, 2)] if part == 0 else ref.at[pl.ds(2 * u, 2), pl.ds(part + 1, 1)]

    def landed(slot, u, part, group):
        return blocks(landing[slot][group], u % (units(part) // 2), part)

    def x_copy(u, part, to_right, group):
        n, slot = (0, 0) if to_right else (1, 2)
        device = {"head": right if to_right else left}
        dst = landed(slot, u, part, group)
        return remote(blocks(xs, u, part), dst, x_ss.at[n, u, part], x_rs.at[slot, u, part], device)

    def x_send(u, part):
        for group in range(2):

            @pl.when(u // (units(part) // 2) == group)
            def _():
                x_copy(u, part, True, group).start()
                x_copy(u, part, False, group).start()

    def x_recv(slot, u, part, group):
        dst = landed(slot, u, part, group)
        return remote(blocks(xs, u, part), dst, f_ss.at[u, part], x_rs.at[slot, u, part], {"head": right})

    def x_forward(u, part, to_right, group):
        device = {"head": right if to_right else left}
        src = landed(0 if to_right else 2, u, part, group)
        dst = landed(1, u, part, group)
        return remote(src, dst, f_ss.at[u, part], x_rs.at[1, u, part], device)

    def each_unit(part, group, act):
        count = units(part) // 2

        def step(n, _):
            act(group * count + n)
            return 0

        lax.fori_loop(0, count, step, 0)

    def forward(part, group):
        def act(u):
            x_recv(0, u, part, group).wait_recv()
            x_recv(2, u, part, group).wait_recv()

            @pl.when(u % 2 == 0)
            def _():
                x_forward(u, part, True, group).start()

            @pl.when(u % 2 == 1)
            def _():
                x_forward(u, part, False, group).start()

        each_unit(part, group, act)

    def attend(key_parts, value_parts, query):
        scores = []
        for keys, allowed in key_parts:
            part = dot(keys, query, NT) * scale
            scores.append(part if allowed is None else jnp.where(allowed, part, NEG))
        top = functools.reduce(jnp.maximum, [jnp.max(part, axis=0, keepdims=True) for part in scores])
        weights = [jnp.exp2(part - top) for part in scores]
        total = functools.reduce(jnp.add, [jnp.sum(part, axis=0, keepdims=True) for part in weights])
        numer = functools.reduce(
            jnp.add, [dot(values, part.astype(BF16), TN) for values, part in zip(value_parts, weights)]
        )
        return numer * (1.0 / total), top + jnp.log2(total)

    def lowest(h, with_mate):
        cols = pl.ds(pl.multiple_of(h * HEAD_DIM, HEAD_DIM), HEAD_DIM)
        for n in range(2):
            column = iota((rows, half), 1)
            residue = jnp.where(column < sel_b, 2 * n, 2 * n + 1 - RATE_B * sel_b)
            causal = iota((rows, half), 0) <= RATE_B * column + residue
            key_parts = [(kv[:, cols], causal)]
            value_parts = [vv[:, cols]]
            if with_mate:
                key_parts.append((mkv[0, :, cols], None))
                value_parts.append(mkv[1, :, cols])
            result, level = attend(key_parts, value_parts, qp[n * half : (n + 1) * half, cols])
            for t in range(2):
                part = slice(t * sel_b, (t + 1) * sel_b)
                oa[h, 2 * n + t] = result[:, part]
                la[h, 2 * n + t] = jnp.broadcast_to(level[:, part], (8, sel_b))

    def zg(t, src):
        return remote(ckv.at[src], ckv.at[src], zg_ss.at[t], zg_rs.at[src], along_z(t))

    go_up = jnp.where(z < 2, 6, 5)

    def lowest_level(h, _):
        @pl.when(core == 1)
        def _():
            for n in range(mates // 2):

                @pl.when(h == n * (chunk // HEAD_DIM))
                def _():
                    for m in range(2):
                        mate_copy(2 * n + m, plane(i - 1)).wait_recv()

            lowest(h, True)

        @pl.when(core == 0)
        def _():
            lowest(h, False)

        second, last = late_residues(offs_b[z, h], offs_c[0, h])
        zero_free = jnp.logical_and(second != 0, last != 0)
        one_free = jnp.logical_and(second != 1, last != 1)
        three_free = jnp.logical_and(second != 3, last != 3)
        two_free = jnp.logical_and(second != 2, last != 2)
        xs[h, 0] = oa[h, jnp.where(zero_free, 0, jnp.where(one_free, 1, 2))].T.astype(BF16)
        xs[h, 1] = oa[h, jnp.where(three_free, 3, jnp.where(two_free, 2, 1))].T.astype(BF16)
        x_send(h, 0)

        @pl.when(jnp.logical_and(h == 0, jnp.logical_and(greeter, z > 0)))
        def _():
            pl.semaphore_wait(barrier, z)

            def down(t):
                pl.semaphore_signal(plane_in, 1, device_id=along_z(t), device_id_type=MESH)

            each_plane(lambda t: t < z, down)

        @pl.when(jnp.logical_and(h == go_up - 1, greeter))
        def _():
            @pl.when(z < nz - 1)
            def _():
                pl.semaphore_wait(plane_in, nz - 1 - z)

            def tell(d, _):
                pl.semaphore_signal(all_in, 1, device_id=plane((i + d) % heads), device_id_type=MESH)
                return 0

            lax.fori_loop(1, heads, tell, 0)

        @pl.when(h == go_up)
        def _():
            def wait_c(d, _):
                p1c(i, (i + d) % heads).wait_recv()
                return 0

            lax.fori_loop(1, heads, wait_c, 0)
            for j in range(heads):
                ckv[z, j * sel_c : (j + 1) * sel_c, :] = rc1c[j, :, HEAD_DIM:]

            @pl.when(jnp.logical_not(greeter))
            def _():
                pl.semaphore_wait(all_in, 1)

            each_plane(lambda t: t > z, lambda t: zg(t, z).start())

        return 0

    lax.fori_loop(0, heads, lowest_level, 0)


    forward(0, 0)

    def wait_b(d, _):
        p1b(i, (i + d) % heads).wait_recv()
        return 0

    lax.fori_loop(1, heads, wait_b, 0)

    def rb(j, src):
        return remote(rbst.at[j], rbrc.at[src], rb_ss.at[j], rb_rs.at[src], plane(j))

    def rc(j, src):
        return remote(rcst.at[j], rcrc.at[src], rc_ss.at[j], rc_rs.at[src], plane(j))

    def field_b(first, last, n):
        part = rc1b[first:last, :, n * HEAD_DIM : (n + 1) * HEAD_DIM]
        return part.reshape((last - first) * sel_b, HEAD_DIM)

    for pair in range(heads // 2):
        first = 2 * pair
        block = 2 * sel_b
        causal = iota((block, block), 0) <= iota((block, block), 1)
        key_parts = [(field_b(first, first + 2, 1), causal)]
        value_parts = [field_b(first, first + 2, 2)]
        if pair:
            key_parts.append((field_b(0, first, 1), None))
            value_parts.append(field_b(0, first, 2))
        result, level = attend(key_parts, value_parts, field_b(first, first + 2, 0))
        stats = stat_rows(16, level)
        for n in range(2):
            cols = slice(n * sel_b, (n + 1) * sel_b)
            rbst[first + n, :HEAD_DIM] = result[:, cols].astype(BF16)
            rbst[first + n, HEAD_DIM:] = stats[:, cols].astype(BF16)

            @pl.when(first + n != i)
            def _():
                rb(first + n, i).start()

    rbrc[i] = rbst[i]
    forward(0, 1)


    def level_of(field):
        return jnp.sum(field[HEAD_DIM : HEAD_DIM + 8].astype(F32), axis=0, keepdims=True)

    def merge(h, residue, others):
        level_a = la[h, residue][0:1]
        peak = functools.reduce(jnp.maximum, [level for _, level in others], level_a)
        factors = [jnp.exp2(level - peak) for level in [level_a] + [level for _, level in others]]
        share = 1.0 / functools.reduce(jnp.add, factors)
        numer = (factors[0] * share) * oa[h, residue]
        for (field, _), factor in zip(others, factors[1:]):
            numer = numer + (factor * share) * field
        return numer.T.astype(BF16)

    def merge_second(h, _):
        @pl.when(h != i)
        def _():
            rb(i, h).wait_recv()

        b = offs_b[z, h]
        second, _ = late_residues(b, offs_c[0, h])
        level_b = jnp.where(second == b, level_of(rbrc[h]), NEG)
        xs[h, 2] = merge(h, second, [(rbrc[h, :HEAD_DIM].astype(F32), level_b)])

        @pl.when(h % 2 == 1)
        def _():
            x_send(h // 2, 1)

        return 0

    lax.fori_loop(0, heads, merge_second, 0)

    each_plane(lambda t: t < z, lambda t: zg(z, t).wait_recv())
    count_c = heads * sel_c
    keys_c = ckv[:, :, :HEAD_DIM].reshape(nz * count_c, HEAD_DIM)
    values_c = ckv[:, :, HEAD_DIM:].reshape(nz * count_c, HEAD_DIM)
    query_c = rc1c[:, :, :HEAD_DIM].reshape(count_c, HEAD_DIM)
    shape_c = (nz * count_c, count_c)
    allowed_c = iota(shape_c, 0) <= iota(shape_c, 1) + z * count_c
    result, level = attend([(keys_c, allowed_c)], [values_c], query_c)
    flat = jnp.concatenate([result.T, stat_rows(HEAD_DIM, level).T], axis=1).astype(BF16)
    rcst[...] = flat.reshape(heads, sel_c, 2 * HEAD_DIM)
    rcrc[i] = rcst[i]

    def send_rc(d, _):
        rc((i + d) % heads, i).start()
        return 0

    lax.fori_loop(1, heads, send_rc, 0)


    def merge_last(h, _):
        @pl.when(h != i)
        def _():
            rc(i, h).wait_recv()

        b = offs_b[z, h]
        c = offs_c[0, h]
        _, last = late_residues(b, c)
        spot = lax.div(c, RATE_B)
        apart = top_stride // RATE_B
        put = one_hot((sel_c, sel_b), iota((sel_c, sel_b), 1) == apart * iota((sel_c, sel_b), 0) + spot)
        from_c = dot(rcrc[h], put, TN)
        level_b = jnp.where(last == b, level_of(rbrc[h]), NEG)
        level_c = jnp.where(lax.rem(iota((1, sel_b), 1), apart) == spot, level_of(from_c), NEG)
        xs[h, 3] = merge(h, last, [(rbrc[h, :HEAD_DIM].astype(F32), level_b), (from_c[:HEAD_DIM], level_c)])

        @pl.when(h % 2 == 1)
        def _():
            x_send(h // 2, 2)

        return 0

    lax.fori_loop(0, heads, merge_last, 0)
    forward(1, 0)
    forward(1, 1)

    own_table.wait()
    for d in range(1, 4):
        table_copy(d).wait_recv()
    tables = [pltpu.make_async_copy(orc.at[d - 1], osm.at[d], os_s.at[d]) for d in range(1, 4)]
    for copy in tables:
        copy.start()
    for copy in tables:
        copy.wait()
    loads[3].wait()

    def project(d, ref, first, count, fresh, final=False):
        def place(n, _):
            h = first + n
            cols = pl.ds(pl.multiple_of(h * HEAD_DIM, HEAD_DIM), HEAD_DIM)
            for r in range(RATE_B):
                att[d, r * sel_b : (r + 1) * sel_b, cols] = ref[n, place_of(r, osm[d, h, 0], osm[d, h, 1])]
            return 0

        lax.fori_loop(0, count, place, 0)
        group = (y + ny - d) % ny
        depth = count * HEAD_DIM
        at = pl.multiple_of(group * width + first * HEAD_DIM, HEAD_DIM)

        def columns(n, _):
            cols = pl.ds(pl.multiple_of(n * chunk, chunk), chunk)
            part = dot(att[d, :, first * HEAD_DIM : first * HEAD_DIM + depth], wv[pl.ds(at, depth), cols])
            if fresh:
                acc[:, cols] = part
            elif final:
                total = acc[:, cols] + part
                for t in range(chunk // 128):
                    for r in range(RATE_B):
                        block = total[r * sel_b : (r + 1) * sel_b, t * 128 : (t + 1) * 128]
                        nat[n, t, pl.ds(r, sel_b, stride=RATE_B), :] = block
                out[:, cols] = jnp.concatenate([nat[n, t, :rows] for t in range(chunk // 128)], axis=1).astype(BF16)
            else:
                acc[:, cols] += part
            return 0

        lax.fori_loop(0, width // chunk, columns, 0)

    project(0, xs, 0, heads, True)
    for group in range(2):
        forward(2, group)
        project(1, from_left0 if group == 0 else from_left1, group * few, few, False)
        project(3, from_right0 if group == 0 else from_right1, group * few, few, False)
    @pl.when(core == 0)
    def _():
        for n in range(mates):
            mate_copy(n, plane(i + 1)).wait_send()

    for d in range(1, 4):
        table_copy(d).wait_send()

    def sent_plane(d, _):
        j = (i + d) % heads
        p1c(j, i).wait_send()
        p1b(j, i).wait_send()
        rb(j, i).wait_send()
        rc(j, i).wait_send()
        return 0

    lax.fori_loop(1, heads, sent_plane, 0)

    each_plane(lambda t: t > z, lambda t: zg(t, z).wait_send())

    def sent_y(u, part):
        x_copy(u, part, True, 0).wait_send()
        x_copy(u, part, False, 0).wait_send()
        x_forward(u, part, True, 0).wait_send()

    for group in range(2):
        if group == 1:
            for part in range(3):
                for half_of in range(2):
                    each_unit(part, half_of, lambda u, part=part: sent_y(u, part))
        for part in range(3):
            each_unit(part, group, lambda u, part=part: x_recv(1, u, part, group).wait_recv())
        project(2, landing[1][group], group * few, few, False, group == 1)


def shards(queries, keys, values, offsets_b, offsets_c, out_weight):
    rows, width = queries.shape
    depth, features = out_weight.shape
    heads = width // HEAD_DIM
    nz = lax.axis_size("seq") // heads
    ny = lax.axis_size("head")
    sel_b = rows // RATE_B
    sel_c = rows // (lax.axis_size("seq") // 2)
    three = 3 * HEAD_DIM
    dma = pltpu.SemaphoreType.DMA
    hbm = pl.BlockSpec(memory_space=pl.ANY)
    smem = pl.BlockSpec(memory_space=pltpu.SMEM)
    scratch = [
        pltpu.VMEM((rows, width), BF16),
        pltpu.VMEM((rows, width), BF16),
        pltpu.VMEM((rows, width), BF16),
        pltpu.VMEM((2, rows, width), BF16),
        pltpu.VMEM((depth, features), BF16),
        pltpu.VMEM((rows, width), BF16),
        *[pltpu.VMEM((heads, rows + sel_b // 4, HEAD_DIM), F32) for _ in range(3)],
        pltpu.VMEM((features // 256, 2, rows + 8, 128), F32),
        pltpu.VMEM((heads, sel_b, three), BF16),
        pltpu.VMEM((heads, sel_c, three), BF16),
        pltpu.VMEM((heads, sel_b, three), BF16),
        pltpu.VMEM((heads, sel_c, three), BF16),
        pltpu.VMEM((nz, heads * sel_c, 2 * HEAD_DIM), BF16),
        pltpu.VMEM((heads, RATE_B, HEAD_DIM, sel_b), F32),
        pltpu.VMEM((heads, RATE_B, 8, sel_b), F32),
        pltpu.VMEM((heads, HEAD_DIM + 16, sel_b), BF16),
        pltpu.VMEM((heads, HEAD_DIM + 16, sel_b), BF16),
        pltpu.VMEM((heads, sel_c, 2 * HEAD_DIM), BF16),
        pltpu.VMEM((heads, sel_c, 2 * HEAD_DIM), BF16),
        pltpu.VMEM((heads, RATE_B, sel_b, HEAD_DIM), BF16),
        *[pltpu.VMEM((heads // 2, RATE_B, sel_b, HEAD_DIM), BF16) for _ in range(6)],
        pltpu.VMEM((ny, rows, width), BF16),
        pltpu.VMEM((rows, features), F32),
        pltpu.VMEM((heads, 128), jnp.int32),
        pltpu.VMEM((3, heads, 128), jnp.int32),
        pltpu.SMEM((ny, heads, 128), jnp.int32),
        dma((4,)),
        dma((2 * (width // 256),)),
        dma((2 * (width // 256),)),
        dma((heads,)),
        dma((heads,)),
        dma((heads,)),
        dma((heads,)),
        dma((nz,)),
        dma((nz,)),
        dma((heads,)),
        dma((heads,)),
        dma((heads,)),
        dma((heads,)),
        dma((2, heads, 3)),
        dma((3, heads, 3)),
        dma((heads, 3)),
        dma((3,)),
        dma((3,)),
        dma((ny,)),
        *[pltpu.SemaphoreType.REGULAR for _ in range(3)],
    ]
    return pl.pallas_call(
        kernel,
        out_shape=jax.ShapeDtypeStruct((rows, features), BF16),
        in_specs=[hbm, hbm, hbm, smem, smem, hbm],
        out_specs=pl.BlockSpec(memory_space=pltpu.VMEM),
        scratch_shapes=scratch,
        compiler_params=pltpu.CompilerParams(
            collective_id=0, has_side_effects=True, vmem_limit_bytes=52 * 2**20
        ),
    )(queries, keys, values, offsets_b, offsets_c.reshape(1, heads), out_weight)


def solution(mesh):
    placed = (
        P("seq", "head"),
        P("seq", "head"),
        P("seq", "head"),
        P(None, "head"),
        P("head"),
        P(None, "head"),
    )
    return jax.shard_map(
        shards, mesh=mesh, in_specs=placed, out_specs=P("seq", "head"), check_vma=False
    )
```

```python
import functools

import jax
import jax.numpy as jnp
from jax import lax
from jax.experimental import pallas as pl
from jax.experimental.pallas import tpu as pltpu
from jax.sharding import PartitionSpec as P

HEAD_DIM = 128
RATE_B = 4
LOG2E = 1.4426950408889634
NEG = -1e30
MESH = pl.DeviceIdType.MESH
F32 = jnp.float32
BF16 = jnp.bfloat16
NN = (((1,), (0,)), ((), ()))
NT = (((1,), (1,)), ((), ()))
TN = (((0,), (0,)), ((), ()))


def dot(a, b, dims=NN):
    return lax.dot_general(a, b, dims, preferred_element_type=F32)


def iota(shape, axis):
    return lax.broadcasted_iota(jnp.int32, shape, axis)


def one_hot(shape, condition):
    return jnp.where(condition, jnp.ones(shape, F32), jnp.zeros(shape, F32)).astype(BF16)


def late_residues(b, c):
    last = lax.rem(c, RATE_B)
    return jnp.where(last == b, lax.rem(b + 1, RATE_B), b), last


def place_of(r, second, last):
    free = r - jnp.where(second < r, 1, 0) - jnp.where(last < r, 1, 0)
    return jnp.where(last == r, 3, jnp.where(second == r, 2, free))


def stat_rows(count, level):
    high = level.astype(BF16).astype(F32)
    rest = level - high
    mid = rest.astype(BF16).astype(F32)
    low = rest - mid
    row = iota((count, level.shape[1]), 0)
    zero = jnp.zeros((count, level.shape[1]), F32)
    return jnp.where(row == 0, high, jnp.where(row == 1, mid, jnp.where(row == 2, low, zero)))


def kernel(
    q_hbm, k_hbm, v_hbm, offs_b, offs_c, w_hbm, out,
    qv, kv, vv, mkv, wv, qp, qf, kf, vf, nat, st1b, st1c, rc1b, rc1c, ckv, oa, la,
    rbst, rbrc, rcst, rcrc, xs, from_left0, from_left1, across0, across1, from_right0, from_right1, att, acc,
    ost, orc, osm,
    ld_s, mate_ss, mate_rs, p1c_ss, p1c_rs, p1b_ss, p1b_rs, zg_ss, zg_rs,
    rb_ss, rb_rs, rc_ss, rc_rs, x_ss, x_rs, f_ss, of_ss, of_rs, os_s, hello, plane_in, all_in,
):
    rows, width = qv.shape
    heads = width // HEAD_DIM
    half = rows // 2
    sel_b = rows // RATE_B
    sel_c = st1c.shape[1]
    top_stride = rows // sel_c
    scale = HEAD_DIM**-0.5 * LOG2E

    s = lax.axis_index("seq")
    y = lax.axis_index("head")
    ny = lax.axis_size("head")
    nz = lax.axis_size("seq") // heads
    z = s // heads
    i = s % heads
    core = s % 2
    right = (y + 1) % ny
    left = (y + ny - 1) % ny

    def plane(j):
        return {"seq": z * heads + j}

    def along_z(t):
        return {"seq": t * heads + i}

    def remote(src, dst, ssem, rsem, device):
        return pltpu.make_async_remote_copy(
            src_ref=src, dst_ref=dst, send_sem=ssem, recv_sem=rsem, device_id=device, device_id_type=MESH
        )

    chunk = 256
    loads = [
        pltpu.make_async_copy(src, dst, ld_s.at[n])
        for n, (src, dst) in enumerate(((q_hbm, qv), (k_hbm, kv), (v_hbm, vv), (w_hbm, wv)))
    ]
    for copy in loads[:3]:
        copy.start()

    barrier = pltpu.get_barrier_semaphore()
    greeter = i == 2 * y
    peers = (heads - 1) + (ny - 1)
    ckv[...] = jnp.zeros(ckv.shape, BF16)

    def greet_plane(d, _):
        j = (i + d) % heads

        @pl.when(jnp.logical_or(greeter, j != 2 * y))
        def _():
            pl.semaphore_signal(barrier, 1, device_id=plane(j), device_id_type=MESH)

        return 0

    def each_plane(condition, act):
        def step(t, _):
            pl.when(condition(t))(lambda: act(t))
            return 0

        lax.fori_loop(0, nz, step, 0)

    def each_group(act):
        for d in range(1, 4):
            act((y + d) % ny)

    def greet_group(other):
        @pl.when(jnp.logical_or(greeter, i != 2 * other))
        def _():
            pl.semaphore_signal(barrier, 1, device_id={"head": other}, device_id_type=MESH)

    each_group(greet_group)
    lax.fori_loop(1, heads, greet_plane, 0)

    @pl.when(greeter)
    def _():
        def up(t):
            pl.semaphore_signal(barrier, 1, device_id=along_z(t), device_id_type=MESH)

        each_plane(lambda t: t > z, up)

    table = jnp.zeros((heads, 128), jnp.int32)
    for h in range(heads):
        second, last = late_residues(offs_b[z, h], offs_c[0, h])
        pair = jnp.where(iota((heads, 128), 1) == 0, second, last)
        table = jnp.where(iota((heads, 128), 0) == h, pair, table)
    ost[...] = table
    own_table = pltpu.make_async_copy(ost, osm.at[0], os_s.at[0])
    own_table.start()

    for copy, field, wide in zip(loads, (qv, kv, vv), (qf, kf, vf)):
        copy.wait()
        for h in range(heads):
            wide[h, :rows] = field[:, h * HEAD_DIM : (h + 1) * HEAD_DIM].astype(F32)

    def pick(j, _):
        b = offs_b[z, j]
        c = offs_c[0, j]
        cols = pl.ds(pl.multiple_of(j * HEAD_DIM, HEAD_DIM), HEAD_DIM)
        for n, wide in enumerate((qf, kf, vf)):
            part = slice(n * HEAD_DIM, (n + 1) * HEAD_DIM)
            st1c[j, :, part] = wide[j, pl.ds(c, sel_c, stride=top_stride), :].astype(BF16)
            st1b[j, :, part] = wide[j, pl.ds(b, sel_b, stride=RATE_B), :].astype(BF16)
        for r in range(RATE_B):
            qp[r * sel_b : (r + 1) * sel_b, cols] = qf[j, pl.ds(r, sel_b, stride=RATE_B), :].astype(BF16)
        return 0

    lax.fori_loop(0, heads, pick, 0)

    @pl.when(jnp.logical_not(greeter))
    def _():
        pl.semaphore_wait(barrier, peers)
        pl.semaphore_signal(hello, 1, device_id=plane(2 * y), device_id_type=MESH)

        def say(other):
            @pl.when(i == 2 * other)
            def _():
                pl.semaphore_signal(hello, 1, device_id={"head": other}, device_id_type=MESH)

        each_group(say)

    @pl.when(greeter)
    def _():
        pl.semaphore_wait(hello, peers)

    def mate_copy(n, device):
        cols = pl.ds((n // 2) * chunk, chunk)
        src, dst = (kv, vv)[n % 2], mkv.at[n % 2]
        return remote(src.at[:, cols], dst.at[:, cols], mate_ss.at[n], mate_rs.at[n], device)

    mates = 2 * (width // chunk)

    def mate_start(first, last):
        @pl.when(core == 0)
        def _():
            for n in range(first, last):
                mate_copy(n, plane(i + 1)).start()

    mate_start(0, 2)

    def table_copy(d):
        return remote(ost, orc.at[d - 1], of_ss.at[d - 1], of_rs.at[d - 1], {"head": (y + d) % ny})

    def p1c(j, src):
        return remote(st1c.at[j], rc1c.at[src], p1c_ss.at[j], p1c_rs.at[src], plane(j))

    def p1b(j, src):
        return remote(st1b.at[j], rc1b.at[src], p1b_ss.at[j], p1b_rs.at[src], plane(j))

    def send_c(d, _):
        p1c((i + d) % heads, i).start()
        return 0

    def send_b(d, _):
        p1b((i + d) % heads, i).start()
        return 0

    lax.fori_loop(1, heads, send_c, 0)
    lax.fori_loop(1, heads, send_b, 0)
    mate_start(2, mates)
    for d in range(1, 4):
        table_copy(d).start()
    loads[3].start()
    rc1b[i] = st1b[i]
    rc1c[i] = st1c[i]

    landing = ((from_left0, from_left1), (across0, across1), (from_right0, from_right1))
    few = heads // 2

    def units(part):
        return heads if part == 0 else few

    def blocks(ref, u, part):
        return ref.at[u, pl.ds(0, 2)] if part == 0 else ref.at[pl.ds(2 * u, 2), pl.ds(part + 1, 1)]

    def landed(slot, u, part, group):
        return blocks(landing[slot][group], u % (units(part) // 2), part)

    def x_copy(u, part, to_right, group):
        n, slot = (0, 0) if to_right else (1, 2)
        device = {"head": right if to_right else left}
        dst = landed(slot, u, part, group)
        return remote(blocks(xs, u, part), dst, x_ss.at[n, u, part], x_rs.at[slot, u, part], device)

    def x_send(u, part):
        for group in range(2):

            @pl.when(u // (units(part) // 2) == group)
            def _():
                x_copy(u, part, True, group).start()
                x_copy(u, part, False, group).start()

    def x_recv(slot, u, part, group):
        dst = landed(slot, u, part, group)
        return remote(blocks(xs, u, part), dst, f_ss.at[u, part], x_rs.at[slot, u, part], {"head": right})

    def x_forward(u, part, to_right, group):
        device = {"head": right if to_right else left}
        src = landed(0 if to_right else 2, u, part, group)
        dst = landed(1, u, part, group)
        return remote(src, dst, f_ss.at[u, part], x_rs.at[1, u, part], device)

    def each_unit(part, group, act):
        count = units(part) // 2

        def step(n, _):
            act(group * count + n)
            return 0

        lax.fori_loop(0, count, step, 0)

    def forward(part, group):
        def act(u):
            x_recv(0, u, part, group).wait_recv()
            x_recv(2, u, part, group).wait_recv()

            @pl.when(u % 2 == 0)
            def _():
                x_forward(u, part, True, group).start()

            @pl.when(u % 2 == 1)
            def _():
                x_forward(u, part, False, group).start()

        each_unit(part, group, act)

    def attend(key_parts, value_parts, query):
        scores = []
        for keys, allowed in key_parts:
            part = dot(keys, query, NT) * scale
            scores.append(part if allowed is None else jnp.where(allowed, part, NEG))
        top = functools.reduce(jnp.maximum, [jnp.max(part, axis=0, keepdims=True) for part in scores])
        weights = [jnp.exp2(part - top) for part in scores]
        total = functools.reduce(jnp.add, [jnp.sum(part, axis=0, keepdims=True) for part in weights])
        numer = functools.reduce(
            jnp.add, [dot(values, part.astype(BF16), TN) for values, part in zip(value_parts, weights)]
        )
        return numer * (1.0 / total), top + jnp.log2(total)

    def lowest(h, with_mate):
        cols = pl.ds(pl.multiple_of(h * HEAD_DIM, HEAD_DIM), HEAD_DIM)
        for n in range(2):
            column = iota((rows, half), 1)
            residue = jnp.where(column < sel_b, 2 * n, 2 * n + 1 - RATE_B * sel_b)
            causal = iota((rows, half), 0) <= RATE_B * column + residue
            key_parts = [(kv[:, cols], causal)]
            value_parts = [vv[:, cols]]
            if with_mate:
                key_parts.append((mkv[0, :, cols], None))
                value_parts.append(mkv[1, :, cols])
            result, level = attend(key_parts, value_parts, qp[n * half : (n + 1) * half, cols])
            for t in range(2):
                part = slice(t * sel_b, (t + 1) * sel_b)
                oa[h, 2 * n + t] = result[:, part]
                la[h, 2 * n + t] = jnp.broadcast_to(level[:, part], (8, sel_b))

    def zg(t, src):
        return remote(ckv.at[src], ckv.at[src], zg_ss.at[t], zg_rs.at[src], along_z(t))

    go_up = jnp.where(z < 2, 6, 5)

    def lowest_level(h, _):
        @pl.when(core == 1)
        def _():
            for n in range(mates // 2):

                @pl.when(h == n * (chunk // HEAD_DIM))
                def _():
                    for m in range(2):
                        mate_copy(2 * n + m, plane(i - 1)).wait_recv()

            lowest(h, True)

        @pl.when(core == 0)
        def _():
            lowest(h, False)

        second, last = late_residues(offs_b[z, h], offs_c[0, h])
        zero_free = jnp.logical_and(second != 0, last != 0)
        one_free = jnp.logical_and(second != 1, last != 1)
        three_free = jnp.logical_and(second != 3, last != 3)
        two_free = jnp.logical_and(second != 2, last != 2)
        xs[h, 0] = oa[h, jnp.where(zero_free, 0, jnp.where(one_free, 1, 2))].T.astype(BF16)
        xs[h, 1] = oa[h, jnp.where(three_free, 3, jnp.where(two_free, 2, 1))].T.astype(BF16)
        x_send(h, 0)

        @pl.when(jnp.logical_and(h == 0, jnp.logical_and(greeter, z > 0)))
        def _():
            pl.semaphore_wait(barrier, z)

            def down(t):
                pl.semaphore_signal(plane_in, 1, device_id=along_z(t), device_id_type=MESH)

            each_plane(lambda t: t < z, down)

        @pl.when(jnp.logical_and(h == go_up - 1, greeter))
        def _():
            @pl.when(z < nz - 1)
            def _():
                pl.semaphore_wait(plane_in, nz - 1 - z)

            def tell(d, _):
                pl.semaphore_signal(all_in, 1, device_id=plane((i + d) % heads), device_id_type=MESH)
                return 0

            lax.fori_loop(1, heads, tell, 0)

        @pl.when(h == go_up)
        def _():
            def wait_c(d, _):
                p1c(i, (i + d) % heads).wait_recv()
                return 0

            lax.fori_loop(1, heads, wait_c, 0)
            for j in range(heads):
                ckv[z, j * sel_c : (j + 1) * sel_c, :] = rc1c[j, :, HEAD_DIM:]

            @pl.when(jnp.logical_not(greeter))
            def _():
                pl.semaphore_wait(all_in, 1)

            each_plane(lambda t: t > z, lambda t: zg(t, z).start())

        return 0

    lax.fori_loop(0, heads, lowest_level, 0)


    forward(0, 0)

    def wait_b(d, _):
        p1b(i, (i + d) % heads).wait_recv()
        return 0

    lax.fori_loop(1, heads, wait_b, 0)

    def rb(j, src):
        return remote(rbst.at[j], rbrc.at[src], rb_ss.at[j], rb_rs.at[src], plane(j))

    def rc(j, src):
        return remote(rcst.at[j], rcrc.at[src], rc_ss.at[j], rc_rs.at[src], plane(j))

    def field_b(first, last, n):
        part = rc1b[first:last, :, n * HEAD_DIM : (n + 1) * HEAD_DIM]
        return part.reshape((last - first) * sel_b, HEAD_DIM)

    for pair in range(heads // 2):
        first = 2 * pair
        block = 2 * sel_b
        causal = iota((block, block), 0) <= iota((block, block), 1)
        key_parts = [(field_b(first, first + 2, 1), causal)]
        value_parts = [field_b(first, first + 2, 2)]
        if pair:
            key_parts.append((field_b(0, first, 1), None))
            value_parts.append(field_b(0, first, 2))
        result, level = attend(key_parts, value_parts, field_b(first, first + 2, 0))
        stats = stat_rows(16, level)
        for n in range(2):
            cols = slice(n * sel_b, (n + 1) * sel_b)
            rbst[first + n, :HEAD_DIM] = result[:, cols].astype(BF16)
            rbst[first + n, HEAD_DIM:] = stats[:, cols].astype(BF16)

            @pl.when(first + n != i)
            def _():
                rb(first + n, i).start()

    rbrc[i] = rbst[i]
    forward(0, 1)


    def level_of(field):
        return jnp.sum(field[HEAD_DIM : HEAD_DIM + 8].astype(F32), axis=0, keepdims=True)

    def merge(h, residue, others):
        level_a = la[h, residue][0:1]
        peak = functools.reduce(jnp.maximum, [level for _, level in others], level_a)
        factors = [jnp.exp2(level - peak) for level in [level_a] + [level for _, level in others]]
        share = 1.0 / functools.reduce(jnp.add, factors)
        numer = (factors[0] * share) * oa[h, residue]
        for (field, _), factor in zip(others, factors[1:]):
            numer = numer + (factor * share) * field
        return numer.T.astype(BF16)

    def merge_second(h, _):
        @pl.when(h != i)
        def _():
            rb(i, h).wait_recv()

        b = offs_b[z, h]
        second, _ = late_residues(b, offs_c[0, h])
        level_b = jnp.where(second == b, level_of(rbrc[h]), NEG)
        xs[h, 2] = merge(h, second, [(rbrc[h, :HEAD_DIM].astype(F32), level_b)])

        @pl.when(h % 2 == 1)
        def _():
            x_send(h // 2, 1)

        return 0

    lax.fori_loop(0, heads, merge_second, 0)

    each_plane(lambda t: t < z, lambda t: zg(z, t).wait_recv())
    count_c = heads * sel_c
    keys_c = ckv[:, :, :HEAD_DIM].reshape(nz * count_c, HEAD_DIM)
    values_c = ckv[:, :, HEAD_DIM:].reshape(nz * count_c, HEAD_DIM)
    query_c = rc1c[:, :, :HEAD_DIM].reshape(count_c, HEAD_DIM)
    shape_c = (nz * count_c, count_c)
    allowed_c = iota(shape_c, 0) <= iota(shape_c, 1) + z * count_c
    result, level = attend([(keys_c, allowed_c)], [values_c], query_c)
    flat = jnp.concatenate([result.T, stat_rows(HEAD_DIM, level).T], axis=1).astype(BF16)
    rcst[...] = flat.reshape(heads, sel_c, 2 * HEAD_DIM)
    rcrc[i] = rcst[i]

    def send_rc(d, _):
        rc((i + d) % heads, i).start()
        return 0

    lax.fori_loop(1, heads, send_rc, 0)


    def merge_last(h, _):
        @pl.when(h != i)
        def _():
            rc(i, h).wait_recv()

        b = offs_b[z, h]
        c = offs_c[0, h]
        _, last = late_residues(b, c)
        spot = lax.div(c, RATE_B)
        apart = top_stride // RATE_B
        put = one_hot((sel_c, sel_b), iota((sel_c, sel_b), 1) == apart * iota((sel_c, sel_b), 0) + spot)
        from_c = dot(rcrc[h], put, TN)
        level_b = jnp.where(last == b, level_of(rbrc[h]), NEG)
        level_c = jnp.where(lax.rem(iota((1, sel_b), 1), apart) == spot, level_of(from_c), NEG)
        xs[h, 3] = merge(h, last, [(rbrc[h, :HEAD_DIM].astype(F32), level_b), (from_c[:HEAD_DIM], level_c)])

        @pl.when(h % 2 == 1)
        def _():
            x_send(h // 2, 2)

        return 0

    lax.fori_loop(0, heads, merge_last, 0)
    forward(1, 0)
    forward(1, 1)

    own_table.wait()
    for d in range(1, 4):
        table_copy(d).wait_recv()
    tables = [pltpu.make_async_copy(orc.at[d - 1], osm.at[d], os_s.at[d]) for d in range(1, 4)]
    for copy in tables:
        copy.start()
    for copy in tables:
        copy.wait()
    loads[3].wait()

    def project(d, ref, first, count, fresh, final=False):
        def place(n, _):
            h = first + n
            cols = pl.ds(pl.multiple_of(h * HEAD_DIM, HEAD_DIM), HEAD_DIM)
            for r in range(RATE_B):
                att[d, r * sel_b : (r + 1) * sel_b, cols] = ref[n, place_of(r, osm[d, h, 0], osm[d, h, 1])]
            return 0

        lax.fori_loop(0, count, place, 0)
        group = (y + ny - d) % ny
        depth = count * HEAD_DIM
        at = pl.multiple_of(group * width + first * HEAD_DIM, HEAD_DIM)

        def columns(n, _):
            cols = pl.ds(pl.multiple_of(n * chunk, chunk), chunk)
            part = dot(att[d, :, first * HEAD_DIM : first * HEAD_DIM + depth], wv[pl.ds(at, depth), cols])
            if fresh:
                acc[:, cols] = part
            elif final:
                total = acc[:, cols] + part
                for t in range(chunk // 128):
                    for r in range(RATE_B):
                        block = total[r * sel_b : (r + 1) * sel_b, t * 128 : (t + 1) * 128]
                        nat[n, t, pl.ds(r, sel_b, stride=RATE_B), :] = block
                out[:, cols] = jnp.concatenate([nat[n, t, :rows] for t in range(chunk // 128)], axis=1).astype(BF16)
            else:
                acc[:, cols] += part
            return 0

        lax.fori_loop(0, width // chunk, columns, 0)

    project(0, xs, 0, heads, True)
    forward(2, 0)
    project(1, from_left0, 0, few, False)
    forward(2, 1)
    project(3, from_right0, 0, few, False)
    project(1, from_left1, few, few, False)
    project(3, from_right1, few, few, False)
    @pl.when(core == 0)
    def _():
        for n in range(mates):
            mate_copy(n, plane(i + 1)).wait_send()

    for d in range(1, 4):
        table_copy(d).wait_send()

    def sent_plane(d, _):
        j = (i + d) % heads
        p1c(j, i).wait_send()
        p1b(j, i).wait_send()
        rb(j, i).wait_send()
        rc(j, i).wait_send()
        return 0

    lax.fori_loop(1, heads, sent_plane, 0)

    each_plane(lambda t: t > z, lambda t: zg(t, z).wait_send())

    def sent_y(u, part):
        x_copy(u, part, True, 0).wait_send()
        x_copy(u, part, False, 0).wait_send()
        x_forward(u, part, True, 0).wait_send()

    for group in range(2):
        if group == 1:
            for part in range(3):
                for half_of in range(2):
                    each_unit(part, half_of, lambda u, part=part: sent_y(u, part))
        for part in range(3):
            each_unit(part, group, lambda u, part=part: x_recv(1, u, part, group).wait_recv())
        project(2, landing[1][group], group * few, few, False, group == 1)


def shards(queries, keys, values, offsets_b, offsets_c, out_weight):
    rows, width = queries.shape
    depth, features = out_weight.shape
    heads = width // HEAD_DIM
    nz = lax.axis_size("seq") // heads
    ny = lax.axis_size("head")
    sel_b = rows // RATE_B
    sel_c = rows // (lax.axis_size("seq") // 2)
    three = 3 * HEAD_DIM
    dma = pltpu.SemaphoreType.DMA
    hbm = pl.BlockSpec(memory_space=pl.ANY)
    smem = pl.BlockSpec(memory_space=pltpu.SMEM)
    scratch = [
        pltpu.VMEM((rows, width), BF16),
        pltpu.VMEM((rows, width), BF16),
        pltpu.VMEM((rows, width), BF16),
        pltpu.VMEM((2, rows, width), BF16),
        pltpu.VMEM((depth, features), BF16),
        pltpu.VMEM((rows, width), BF16),
        *[pltpu.VMEM((heads, rows + sel_b // 4, HEAD_DIM), F32) for _ in range(3)],
        pltpu.VMEM((features // 256, 2, rows + 8, 128), F32),
        pltpu.VMEM((heads, sel_b, three), BF16),
        pltpu.VMEM((heads, sel_c, three), BF16),
        pltpu.VMEM((heads, sel_b, three), BF16),
        pltpu.VMEM((heads, sel_c, three), BF16),
        pltpu.VMEM((nz, heads * sel_c, 2 * HEAD_DIM), BF16),
        pltpu.VMEM((heads, RATE_B, HEAD_DIM, sel_b), F32),
        pltpu.VMEM((heads, RATE_B, 8, sel_b), F32),
        pltpu.VMEM((heads, HEAD_DIM + 16, sel_b), BF16),
        pltpu.VMEM((heads, HEAD_DIM + 16, sel_b), BF16),
        pltpu.VMEM((heads, sel_c, 2 * HEAD_DIM), BF16),
        pltpu.VMEM((heads, sel_c, 2 * HEAD_DIM), BF16),
        pltpu.VMEM((heads, RATE_B, sel_b, HEAD_DIM), BF16),
        *[pltpu.VMEM((heads // 2, RATE_B, sel_b, HEAD_DIM), BF16) for _ in range(6)],
        pltpu.VMEM((ny, rows, width), BF16),
        pltpu.VMEM((rows, features), F32),
        pltpu.VMEM((heads, 128), jnp.int32),
        pltpu.VMEM((3, heads, 128), jnp.int32),
        pltpu.SMEM((ny, heads, 128), jnp.int32),
        dma((4,)),
        dma((2 * (width // 256),)),
        dma((2 * (width // 256),)),
        dma((heads,)),
        dma((heads,)),
        dma((heads,)),
        dma((heads,)),
        dma((nz,)),
        dma((nz,)),
        dma((heads,)),
        dma((heads,)),
        dma((heads,)),
        dma((heads,)),
        dma((2, heads, 3)),
        dma((3, heads, 3)),
        dma((heads, 3)),
        dma((3,)),
        dma((3,)),
        dma((ny,)),
        *[pltpu.SemaphoreType.REGULAR for _ in range(3)],
    ]
    return pl.pallas_call(
        kernel,
        out_shape=jax.ShapeDtypeStruct((rows, features), BF16),
        in_specs=[hbm, hbm, hbm, smem, smem, hbm],
        out_specs=pl.BlockSpec(memory_space=pltpu.VMEM),
        scratch_shapes=scratch,
        compiler_params=pltpu.CompilerParams(
            collective_id=0, has_side_effects=True, vmem_limit_bytes=52 * 2**20
        ),
    )(queries, keys, values, offsets_b, offsets_c.reshape(1, heads), out_weight)


def solution(mesh):
    placed = (
        P("seq", "head"),
        P("seq", "head"),
        P("seq", "head"),
        P(None, "head"),
        P("head"),
        P(None, "head"),
    )
    return jax.shard_map(
        shards, mesh=mesh, in_specs=placed, out_specs=P("seq", "head"), check_vma=False
    )
```
